32 devices in a mesh: group: 2 (over y), lon: 4 (over z), lat: 2 (over x), section: 2 (over core).
Axes of the slice: x: 2, y: 2, z: 4, core: 2. Of those that a mesh axis runs over, the one named last changes fastest.
Arguments:
- saved_inputs: bfloat16 [2, 4, 16, 64, 256], P('section', 'group', 'lat', 'lon'), parts along dimension 1, may hold values from -6 to 6
- out_cotangent: bfloat16 [4, 16, 64, 256], P('group', 'lat', 'lon'), parts along dimension 0, may hold values from -6 to 6
- land_mask: int32 [16, 64], P('lat', 'lon'), may hold values 0 or 1
- conv_kernel: bfloat16 [2, 7, 7, 256], P('section'), may hold values from -0.875 to 0.875
- conv_bias: float32 [2, 256], P('section'), may hold values from -3 to 3
- norm_gain: float32 [2, 256], P('section'), may hold values from 0.4 to 2.5
- w_in: bfloat16 [2, 256, 1024], P('section'), may hold values from -0.375 to 0.375
- b_in: float32 [2, 1024], P('section'), may hold values from -4 to 4
- w_out: bfloat16 [2, 1024, 256], P('section'), may hold values from -0.1875 to 0.1875
Outputs:
- input_grads: bfloat16 [2, 4, 16, 64, 256], P('section', 'group', 'lat', 'lon'), parts along dimension 1
- grad_w_in: float32 [2, 512, 1024], P('section', 'group'), parts along dimension 1
- grad_w_out: float32 [2, 2048, 256], P('section', 'group'), parts along dimension 1
- grad_kernel: float32 [2, 98, 256], P('section', 'group'), parts along dimension 1
The draws below stay inside these ranges and needn't reach their ends.
There are 2 independent parts, one for each index of `group`. The reference program is written for one: setup_inputs(seed, part) draws one part's arguments, and reference() takes and returns one part's arrays. A program takes and returns all parts, laid end to end along the dimension named above; an argument that names none is the same for every part. Nothing has to cross between parts.
All inputs are finite; a program needn't handle non-finite values. No bound on the sum of `land_mask` on one device may be relied on, other than what follows from the above.
Results may differ from the reference program's by a relative error of at most 0.01.
Values may be sent and summed in bfloat16 or wider, within the bound.
No kernel may reach another device: no remote copies, remote signals or barrier semaphores. Data moves between devices by JAX's collectives and lax.ppermute only.
A program may use at most 64 MiB of HBM per device.

```python
import math
import jax
import jax.numpy as jnp
from jax import lax

C = 256
HID = 1024
MB = 2
NLAT = 16
NLON = 64


def place_ends(drawn, key, smallest, top_value):
    extent = drawn.shape
    index_at = [jax.random.randint(jax.random.fold_in(key, axis), (), 0, extent[axis]) for axis in range(len(extent))]
    drawn = drawn.at[tuple(index_at)].set(smallest)
    longest = extent.index(max(extent))
    index_at[longest] = (index_at[longest] + 1) % extent[longest]
    return drawn.at[tuple(index_at)].set(top_value)


def steps_of(own_key, shape, cuts, least, largest):
    def one(position, shards_of):
        steps = jax.random.uniform(jax.random.fold_in(jax.random.fold_in(own_key, 6), position), (shards_of,), jnp.float32, least / len(cuts), largest / len(cuts))
        return jnp.repeat(jnp.exp(steps), shape[position] // shards_of).reshape((-1,) + (1,) * (len(shape) - position - 1))

    level = one(*cuts[0])
    for cut in cuts[1:]:
        level = level * one(*cut)
    return level


def scatter_about(rng, shape, scale, reach, split=(), held_as=jnp.bfloat16):
    level = steps_of(rng, shape, split, -0.22, 0.18) if split else 1.0
    result = jax.random.normal(rng, shape, jnp.float32) * scale * level
    return jnp.minimum(jnp.maximum(result, -reach), reach).astype(held_as)


def setup_inputs(seed: int = 0, part: int = 0) -> dict:
    seeds = jax.random.split(jax.random.key(seed), 10)
    own_keys = jax.random.split(jax.random.fold_in(seeds[9], part), 10)
    saved_inputs = scatter_about(own_keys[0], (2, MB, NLAT, NLON, C), 1.0, 6.0, ((0, 2), (2, 2), (3, 4)))
    out_cotangent = scatter_about(own_keys[1], (MB, NLAT, NLON, C), 1.0, 6.0, ((1, 2), (2, 4)))
    land_mask = place_ends((jax.random.randint(seeds[2], (NLAT, NLON), 0, 10) < 7).astype(jnp.int32), jax.random.fold_in(seeds[2], 1), 0, 1)
    conv_kernel = scatter_about(seeds[3], (2, 7, 7, C), 49 ** -0.5, 0.875, ((0, 2),))
    conv_bias = scatter_about(seeds[4], (2, C), 0.5, 3.0, ((0, 2),), jnp.float32)
    norm_gain = jnp.clip(jnp.exp(math.log(2.5) - 1.8325814 * jax.random.uniform(seeds[5], (2, C), jnp.float32) ** steps_of(seeds[5], (2, C), ((0, 2),), -0.2, 0.2)), 0.4, 2.5)
    w_in = scatter_about(seeds[6], (2, C, HID), C ** -0.5, 0.375, ((0, 2),))
    b_in = scatter_about(seeds[7], (2, HID), 0.7, 4.0, ((0, 2),), jnp.float32)
    w_out = scatter_about(seeds[8], (2, HID, C), HID ** -0.5, 0.1875, ((0, 2),))
    return {"saved_inputs": saved_inputs, "out_cotangent": out_cotangent, "land_mask": land_mask, "conv_kernel": conv_kernel, "conv_bias": conv_bias, "norm_gain": norm_gain, "w_in": w_in, "b_in": b_in, "w_out": w_out}


gelu_k = 0.7978845608028654
gelu_c = 0.044715

def gelu_value(h):
    return 0.5 * h * (1.0 + jnp.tanh(gelu_k * (h + gelu_c * h * h * h)))

def gelu_slope(h):
    tval = jnp.tanh(gelu_k * (h + gelu_c * h * h * h))
    return 0.5 * (1.0 + tval) + 0.5 * h * (1.0 - tval * tval) * gelu_k * (1.0 + 3.0 * gelu_c * h * h)

def widen(field, width):
    padded = jnp.pad(field, ((width, width), (0, 0), (0, 0)))
    return jnp.concatenate([padded[:, -width:], padded, padded[:, :width]], axis=1)

def depthwise(padded, kernel, rows, cols):
    kern = kernel.astype(jnp.float32)
    source = padded.astype(jnp.float32)
    total = jnp.zeros((rows, cols, source.shape[2]), jnp.float32)
    for ka in range(7):
        for kb in range(7):
            total = total + source[ka:ka + rows, kb:kb + cols] * kern[ka, kb]
    return total

def block_backward(field, cot, maskf, kernel, bias, gain, weight_in, bias_in, weight_out):
    rows, cols, chans = field.shape
    padded = widen(field, 3)
    zval = depthwise(padded, kernel, rows, cols) + bias
    centred = zval - lax.optimization_barrier(jnp.mean(zval, axis=-1, keepdims=True))
    rscale = lax.rsqrt(lax.optimization_barrier(jnp.mean(centred * centred, axis=-1, keepdims=True)) + 1e-06)
    zhat = centred * rscale
    normed = (zhat * gain).astype(jnp.bfloat16).reshape(-1, chans)
    hidden = jnp.dot(normed, weight_in, preferred_element_type=jnp.float32) + bias_in
    act = gelu_value(hidden).astype(jnp.bfloat16)
    masked = (cot.astype(jnp.float32) * maskf).astype(jnp.bfloat16)
    flat_g = masked.reshape(-1, chans)
    grad_out = jnp.dot(act.T, flat_g, preferred_element_type=jnp.float32)
    dact = jnp.dot(flat_g, weight_out.T, preferred_element_type=jnp.float32)
    dhid = (dact * gelu_slope(hidden)).astype(jnp.bfloat16)
    grad_in = jnp.dot(normed.T, dhid, preferred_element_type=jnp.float32)
    dnorm = jnp.dot(dhid, weight_in.T, preferred_element_type=jnp.float32).reshape(rows, cols, chans)
    dzh = dnorm * gain
    dzval = rscale * (dzh - lax.optimization_barrier(jnp.mean(dzh, axis=-1, keepdims=True)) - zhat * lax.optimization_barrier(jnp.mean(dzh * zhat, axis=-1, keepdims=True)))
    dzval = dzval.astype(jnp.bfloat16)
    dz32 = dzval.astype(jnp.float32)
    src32 = padded.astype(jnp.float32)
    kgrads = []
    for ka in range(7):
        for kb in range(7):
            kgrads.append(lax.optimization_barrier(jnp.sum(dz32 * src32[ka:ka + rows, kb:kb + cols], axis=(0, 1))))
    grad_k = jnp.stack(kgrads)
    back = depthwise(widen(dzval, 3), kernel[::-1, ::-1], rows, cols)
    dfield = (masked.astype(jnp.float32) + back).astype(jnp.bfloat16)
    return (dfield, grad_in, grad_out, grad_k)

def reference(saved_inputs, out_cotangent, land_mask, conv_kernel, conv_bias, norm_gain, w_in, b_in, w_out):
    maskf = land_mask.astype(jnp.float32)[:, :, None]
    sums_in = [jnp.zeros((C, HID), jnp.float32) for k in range(2)]
    sums_out = [jnp.zeros((HID, C), jnp.float32) for k in range(2)]
    sums_k = [jnp.zeros((49, C), jnp.float32) for k in range(2)]
    grads = [[], []]
    for micro in range(MB):
        cot = out_cotangent[micro]
        for blk in (1, 0):
            cot, g_in, g_out, g_k = block_backward(saved_inputs[blk, micro], cot, maskf, conv_kernel[blk], conv_bias[blk], norm_gain[blk], w_in[blk], b_in[blk], w_out[blk])
            grads[blk].append(cot)
            sums_in[blk] = sums_in[blk] + g_in
            sums_out[blk] = sums_out[blk] + g_out
            sums_k[blk] = sums_k[blk] + g_k
    factor = 1.0 / (MB * NLAT * NLON) ** 0.5
    input_grads = jnp.stack([jnp.stack(grads[0]), jnp.stack(grads[1])])
    return (input_grads, jnp.stack(sums_in) * factor, jnp.stack(sums_out) * factor, jnp.stack(sums_k) * factor)
```

```python
import functools
import jax
import jax.numpy as jnp
from jax import lax
from jax.experimental import pallas as pl
from jax.experimental.pallas import tpu as pltpu
from jax.sharding import PartitionSpec as P

gelu_k = 0.7978845608028654
gelu_c = 0.044715
LANES = 128
HALO = 3
SIDE = 8
F32 = jnp.float32
BF16 = jnp.bfloat16
VMEM_LIMIT = 48 * 1024 * 1024
GATHER_TILES = 8


def call(body, outs, scratch, *args, flops=0):
    moved = sum(a.size * a.dtype.itemsize for a in args)
    moved += sum(o.size * o.dtype.itemsize for o in outs)
    return pl.pallas_call(
        body,
        out_shape=outs,
        in_specs=[pl.BlockSpec(memory_space=pltpu.VMEM)] * len(args),
        out_specs=[pl.BlockSpec(memory_space=pltpu.VMEM)] * len(outs),
        scratch_shapes=scratch,
        compiler_params=pltpu.CompilerParams(vmem_limit_bytes=VMEM_LIMIT),
        cost_estimate=pl.CostEstimate(flops=flops, bytes_accessed=moved, transcendentals=0),
    )(*args)


def like(shape, dtype):
    return jax.ShapeDtypeStruct(shape, dtype)


def nt_dot(left, right):
    return lax.dot_general(left, right, (((1,), (1,)), ((), ())), preferred_element_type=F32)


def tn_dot(left, right):
    return lax.dot_general(left, right, (((0,), (0,)), ((), ())), preferred_element_type=F32)


def gelu_both(h):
    h2 = h * h
    tval = jnp.tanh(h * (gelu_k + (gelu_k * gelu_c) * h2))
    half = 0.5 + 0.5 * tval
    slope = half + (0.5 * h) * (1.0 - tval * tval) * (gelu_k + (3.0 * gelu_k * gelu_c) * h2)
    return h * half, slope


def widen(dst, own, low, high, left, right):
    rows, cols = own.shape[1], own.shape[2]
    dst[:, :HALO, SIDE : SIDE + cols, :] = low[...].astype(F32)
    dst[:, HALO : HALO + rows, SIDE : SIDE + cols, :] = own[...].astype(F32)
    dst[:, HALO + rows :, SIDE : SIDE + cols, :] = high[...].astype(F32)
    dst[:, :, SIDE - HALO : SIDE, :] = left[...].astype(F32)
    dst[:, :, SIDE + cols : SIDE + cols + HALO, :] = right[...].astype(F32)


def depthwise(src, kern, rows, cols, flip, emit):
    micros, chans = src.shape[0], src.shape[3]
    for part in range(chans // LANES):
        lanes = slice(part * LANES, (part + 1) * LANES)
        for micro in range(micros):
            total = jnp.zeros((rows, cols, LANES), F32)
            for kb in range(7):
                begin = SIDE - HALO + kb
                slab = src[micro, :, begin : begin + cols, lanes]
                for ka in range(7):
                    tap = (6 - ka) * 7 + (6 - kb) if flip else ka * 7 + kb
                    total = total + slab[ka : ka + rows] * kern[tap : tap + 1, lanes]
            emit(micro, lanes, total)


def dense_back(masked, slope, zhat, rscale, gain, w_in, w_out):
    dact = nt_dot(masked, w_out)
    dhid = (dact * slope).astype(BF16)
    dzh = nt_dot(dhid, w_in) * gain
    return rscale * (
        dzh
        - jnp.mean(dzh, axis=-1, keepdims=True)
        - zhat * jnp.mean(dzh * zhat, axis=-1, keepdims=True)
    )


def forward_body(
    x, low, high, left, right, masked, kern, bias, gain, w_in, b_in, w_out,
    wide, normed, zhat, rscale, slope, dz, zval,
):
    rows, cols = x.shape[1], x.shape[2]
    widen(wide, x, low, high, left, right)

    def emit(micro, lanes, total):
        cells = rows * cols
        zval[micro * cells : (micro + 1) * cells, lanes] = total.reshape(cells, LANES)

    depthwise(wide, kern, rows, cols, False, emit)
    z = zval[...] + bias[...]
    centred = z - jnp.mean(z, axis=-1, keepdims=True)
    rs = lax.rsqrt(jnp.mean(centred * centred, axis=-1, keepdims=True) + 1e-06)
    zh = centred * rs
    n = (zh * gain[...]).astype(BF16)
    normed[...] = n
    zhat[...] = zh
    rscale[...] = rs
    h = jnp.dot(n, w_in[...], preferred_element_type=F32) + b_in[...]
    _, sl = gelu_both(h)
    slope[...] = sl
    dz[...] = dense_back(masked[...], sl, zh, rs, gain[...], w_in[...], w_out[...]).astype(BF16)


def back_body(masked, slope, zhat, rscale, gain, w_in, w_out, dz):
    dz[...] = dense_back(
        masked[...], slope[...], zhat[...], rscale[...], gain[...], w_in[...], w_out[...]
    ).astype(BF16)


def kernel_grad_body(wide, dz, grad):
    micros, rows, cols, chans = dz.shape
    for part in range(chans // LANES):
        lanes = slice(part * LANES, (part + 1) * LANES)
        for kb in range(7):
            begin = SIDE - HALO + kb
            sums = [None] * 7
            for micro in range(micros):
                own = dz[micro, :, :, lanes].astype(F32)
                slab = wide[micro, :, begin : begin + cols, lanes]
                for ka in range(7):
                    prod = jnp.sum(slab[ka : ka + rows] * own, axis=0)
                    sums[ka] = prod if sums[ka] is None else sums[ka] + prod
            for ka in range(7):
                tap = ka * 7 + kb
                grad[tap : tap + 1, lanes] = jnp.sum(sums[ka], axis=0, keepdims=True)


def input_grad_body(own, low, high, left, right, masked, maskb, kern, dx, dxm, wide):
    rows, cols = own.shape[1], own.shape[2]
    widen(wide, own, low, high, left, right)

    def emit(micro, lanes, total):
        value = (total + masked[micro, :, :, lanes].astype(F32)).astype(BF16)
        dx[micro, :, :, lanes] = value
        dxm[micro, :, :, lanes] = (value.astype(F32) * maskb[...]).astype(BF16)

    depthwise(wide, kern, rows, cols, True, emit)


def weight_grad_body(parts, factor, *refs):
    normed, masked = refs[:parts], refs[parts : 2 * parts]
    w_in, b_in, w_out, grad_in, grad_out = refs[2 * parts :]
    grad_in[...] = jnp.zeros_like(grad_in)
    grad_out[...] = jnp.zeros_like(grad_out)
    for part in range(parts):
        cells = normed[part].shape[0]
        step = min(cells, 256)

        @pl.loop(0, cells // step)
        def _(index):
            at = pl.ds(pl.multiple_of(index * step, step), step)
            n = normed[part][at, :]
            gm = masked[part][at, :]
            h = jnp.dot(n, w_in[...], preferred_element_type=F32) + b_in[...]
            act, slope = gelu_both(h)
            dhid = (nt_dot(gm, w_out[...]) * slope).astype(BF16)
            grad_in[...] += tn_dot(n, dhid)
            grad_out[...] += tn_dot(act.astype(BF16), gm)

    grad_in[...] = grad_in[...] * factor
    grad_out[...] = grad_out[...] * factor


def lat_edges(first, last):
    count = lax.axis_size("lat")
    if count == 1:
        return jnp.zeros_like(last), jnp.zeros_like(first)
    if count == 2:
        index = lax.axis_index("lat")
        got = lax.ppermute(jnp.where(index == 0, last, first), "lat", [(0, 1), (1, 0)])
        none = jnp.zeros_like(got)
        return jnp.where(index == 0, none, got), jnp.where(index == 0, got, none)
    up = [(i, i + 1) for i in range(count - 1)]
    low = lax.ppermute(last, "lat", up)
    return low, lax.ppermute(first, "lat", [(b, a) for a, b in up])


def halo(own):
    low, high = lat_edges(own[:, :HALO], own[:, -HALO:])
    count = lax.axis_size("lon")
    firsts = jnp.concatenate([v[:, :, :HALO] for v in (low, own, high)], axis=1)
    lasts = jnp.concatenate([v[:, :, -HALO:] for v in (low, own, high)], axis=1)
    ring = [(i, (i + 1) % count) for i in range(count)]
    left = lax.ppermute(lasts, "lon", ring)
    right = lax.ppermute(firsts, "lon", [(b, a) for a, b in ring])
    return low, high, left, right


def ring_pieces(value, axis):
    count = lax.axis_size(axis)
    return [value] + [
        lax.ppermute(value, axis, [(i, (i + d) % count) for i in range(count)])
        for d in range(1, count)
    ]


def crossing_pieces(value):
    count = lax.axis_size("lon")
    pieces = []
    for d in range(count):
        pairs = []
        for i in range(count):
            for s in range(2):
                pairs.append((i * 2 + s, ((i + d) % count) * 2 + 1 - s))
        pieces.append(lax.ppermute(value, ("lon", "section"), pairs))
    return pieces


def summed(value):
    for axis in ("lat", "lon"):
        count = lax.axis_size(axis)
        if count & (count - 1):
            value = lax.psum(value, axis)
            continue
        step = 1
        while step < count:
            value = value + lax.ppermute(value, axis, [(i, i ^ step) for i in range(count)])
            step *= 2
    return value


def shards(
    saved_inputs, out_cotangent, land_mask, conv_kernel, conv_bias, norm_gain, w_in, b_in, w_out
):
    micros, rows, cols, chans = out_cotangent.shape
    hidden = w_in.shape[2]
    cells = micros * rows * cols
    shape = (micros, rows, cols, chans)
    wide_shape = (micros, rows + 2 * HALO, SIDE + cols + SIDE, chans)
    flat = (cells, chans)
    tiles = lax.axis_size("lat") * lax.axis_size("lon")
    factor = 1.0 / (cells * tiles) ** 0.5
    section = lax.axis_index("section")
    gather = tiles <= GATHER_TILES

    kern = conv_kernel[0].reshape(49, chans).astype(F32)
    weight_in, weight_out = w_in[0], w_out[0]
    maskf = land_mask.astype(F32)
    maskb = jnp.broadcast_to(maskf[:, :, None], (rows, cols, LANES))
    masked1 = (out_cotangent.astype(F32) * maskf[None, :, :, None]).astype(BF16)

    x = saved_inputs[0]
    wide, normed, zhat, rscale, slope, dz = call(
        forward_body,
        [
            like(wide_shape, F32),
            like(flat, BF16),
            like(flat, F32),
            like((cells, 1), F32),
            like((cells, hidden), F32),
            like(flat, BF16),
        ],
        [pltpu.VMEM(flat, F32)],
        x, *halo(x), masked1.reshape(flat), kern, conv_bias, norm_gain, weight_in, b_in, weight_out,
        flops=6 * cells * chans * hidden + 98 * cells * chans,
    )
    if gather:
        normed_row = jnp.concatenate(ring_pieces(normed, "lon"))
        normed_all = ring_pieces(normed_row, "lat")

    def input_grad(dz, masked):
        dz = dz.reshape(shape)
        edges = halo(dz)
        (grad_k,) = call(
            kernel_grad_body, [like((49, chans), F32)], [], wide, dz, flops=98 * cells * chans
        )
        dx, dxm = call(
            input_grad_body,
            [like(shape, BF16), like(shape, BF16)],
            [pltpu.VMEM(wide_shape, F32)],
            dz, *edges, masked, maskb, kern,
            flops=98 * cells * chans,
        )
        return grad_k, dx, dxm

    grad_k1, dx1, dxm1 = input_grad(dz, masked1)
    cross = jnp.where(section == 1, dxm1, masked1).reshape(flat)
    if gather:
        pieces = crossing_pieces(cross)
        masked0 = pieces[0]
        masked_all = ring_pieces(jnp.concatenate(pieces), "lat")
    else:
        masked0 = lax.ppermute(cross, "section", [(0, 1), (1, 0)])
        normed_all, masked_all = [normed], [masked0]
    (dz0,) = call(
        back_body, [like(flat, BF16)], [],
        masked0, slope, zhat, rscale, norm_gain, weight_in, weight_out,
        flops=4 * cells * chans * hidden,
    )
    grad_k0, dx0, _ = input_grad(dz0, masked0.reshape(shape))
    grad_k = summed(jnp.where(section == 1, grad_k1, grad_k0)) * factor
    grad_in, grad_out = call(
        functools.partial(weight_grad_body, len(normed_all), factor),
        [like((chans, hidden), F32), like((hidden, chans), F32)],
        [],
        *normed_all, *masked_all, weight_in, b_in, weight_out,
        flops=8 * sum(v.shape[0] for v in normed_all) * chans * hidden,
    )
    if not gather:
        grad_in, grad_out = lax.psum((grad_in, grad_out), ("lon", "lat"))
    results = jnp.where(section == 1, dx1, dx0)
    return results[None], grad_in[None], grad_out[None], grad_k[None]


def solution(mesh):
    in_specs = (
        P("section", "group", "lat", "lon", None),
        P("group", "lat", "lon", None),
        P("lat", "lon"),
        P("section", None, None, None),
        P("section", None),
        P("section", None),
        P("section", None, None),
        P("section", None),
        P("section", None, None),
    )
    out_specs = (
        P("section", "group", "lat", "lon", None),
        P("section", "group", None),
        P("section", "group", None),
        P("section", "group", None),
    )
    return jax.shard_map(shards, mesh=mesh, in_specs=in_specs, out_specs=out_specs, check_vma=False)
```

```python
import functools
import jax
import jax.numpy as jnp
from jax import lax
from jax.experimental import pallas as pl
from jax.experimental.pallas import tpu as pltpu
from jax.sharding import PartitionSpec as P

gelu_k = 0.7978845608028654
gelu_c = 0.044715
LANES = 128
HALO = 3
SIDE = 8
F32 = jnp.float32
BF16 = jnp.bfloat16
VMEM_LIMIT = 16 * 1024 * 1024
GATHER_TILES = 8


def call(body, outs, scratch, *args, micros=1.0, scalars=0, specs=None, limit=VMEM_LIMIT):
    if specs is None:
        specs = [pl.BlockSpec(memory_space=pltpu.SMEM)] * scalars
        specs += [pl.BlockSpec(memory_space=pltpu.VMEM)] * (len(args) - scalars)
    return pl.pallas_call(
        body,
        out_shape=outs,
        in_specs=specs,
        out_specs=[pl.BlockSpec(memory_space=pltpu.VMEM)] * len(outs),
        scratch_shapes=scratch,
        compiler_params=pltpu.CompilerParams(vmem_limit_bytes=limit),
        cost_estimate=pl.CostEstimate(
            flops=int(micros * 1.1e9), bytes_accessed=int(micros * 3.6e6), transcendentals=0
        ),
    )(*args)


def like(shape, dtype):
    return jax.ShapeDtypeStruct(shape, dtype)


def nt_dot(left, right):
    return lax.dot_general(left, right, (((1,), (1,)), ((), ())), preferred_element_type=F32)


def tn_dot(left, right):
    return lax.dot_general(left, right, (((0,), (0,)), ((), ())), preferred_element_type=F32)


def gelu_both(h):
    h2 = h * h
    tval = jnp.tanh(h * (gelu_k + (gelu_k * gelu_c) * h2))
    half = 0.5 + 0.5 * tval
    slope = half + (0.5 * h) * (1.0 - tval * tval) * (gelu_k + (3.0 * gelu_k * gelu_c) * h2)
    return h * half, slope


def widen(dst, own, low, high, left, right):
    rows, cols = own.shape[1], own.shape[2]
    dst[:, :HALO, SIDE : SIDE + cols, :] = low[...].astype(F32)
    dst[:, HALO : HALO + rows, SIDE : SIDE + cols, :] = own[...].astype(F32)
    dst[:, HALO + rows :, SIDE : SIDE + cols, :] = high[...].astype(F32)
    dst[:, :, SIDE - HALO : SIDE, :] = left[...].astype(F32)
    dst[:, :, SIDE + cols : SIDE + cols + HALO, :] = right[...].astype(F32)


def depthwise(src, kern, rows, cols, begin, flip, emit):
    micros, chans = src.shape[0], src.shape[3]
    chunk = 8 if cols > 8 else 16
    chunk = chunk if rows % chunk == 0 else rows
    for part in range(chans // LANES):
        lanes = slice(part * LANES, (part + 1) * LANES)
        for micro in range(micros):
            for first in range(0, rows, chunk):
                total = jnp.zeros((chunk, cols, LANES), F32)
                for kb in range(7):
                    at = slice(begin + kb, begin + kb + cols)
                    slab = src[micro, first : first + chunk + 2 * HALO, at, lanes]
                    for ka in range(7):
                        tap = (6 - ka) * 7 + (6 - kb) if flip else ka * 7 + kb
                        total = total + slab[ka : ka + chunk] * kern[tap : tap + 1, lanes]
                emit(micro, first, chunk, lanes, total)


def dense_back(masked, slope, zhat, rscale, gain, w_in, w_out):
    dact = nt_dot(masked, w_out)
    dhid = (dact * slope).astype(BF16)
    dzh = nt_dot(dhid, w_in) * gain
    return rscale * (
        dzh
        - jnp.mean(dzh, axis=-1, keepdims=True)
        - zhat * jnp.mean(dzh * zhat, axis=-1, keepdims=True)
    )


def forward_body(
    x, low, high, left, right, masked, kern, bias, gain, w_in, b_in, w_out,
    wide, normed, zhat, rscale, slope, dz, zval,
):
    rows, cols = x.shape[1], x.shape[2]
    widen(wide, x, low, high, left, right)

    def emit(micro, first, chunk, lanes, total):
        at = (micro * rows + first) * cols
        zval[at : at + chunk * cols, lanes] = total.reshape(chunk * cols, LANES)

    depthwise(wide, kern, rows, cols, SIDE - HALO, False, emit)
    z = zval[...] + bias[...]
    centred = z - jnp.mean(z, axis=-1, keepdims=True)
    rs = lax.rsqrt(jnp.mean(centred * centred, axis=-1, keepdims=True) + 1e-06)
    zh = centred * rs
    n = (zh * gain[...]).astype(BF16)
    normed[...] = n
    zhat[...] = zh
    rscale[...] = rs
    h = jnp.dot(n, w_in[...], preferred_element_type=F32) + b_in[...]
    _, sl = gelu_both(h)
    slope[...] = sl
    dz[...] = dense_back(masked[...], sl, zh, rs, gain[...], w_in[...], w_out[...]).astype(BF16)


def back_body(masked, slope, zhat, rscale, gain, w_in, w_out, dz):
    dz[...] = dense_back(
        masked[...], slope[...], zhat[...], rscale[...], gain[...], w_in[...], w_out[...]
    ).astype(BF16)


def kernel_grad_body(first, wide, dz, grad):
    micros, rows, cols, chans = dz.shape
    for part in range(chans // LANES):
        lanes = slice(part * LANES, (part + 1) * LANES)
        for kb in range(7):
            begin = first + kb
            sums = [None] * 7
            for micro in range(micros):
                own = dz[micro, :, :, lanes].astype(F32)
                slab = wide[micro, :, begin : begin + cols, lanes]
                for ka in range(7):
                    prod = jnp.sum(slab[ka : ka + rows] * own, axis=0)
                    sums[ka] = prod if sums[ka] is None else sums[ka] + prod
            for ka in range(7):
                tap = ka * 7 + kb
                grad[tap : tap + 1, lanes] = jnp.sum(sums[ka], axis=0, keepdims=True)


def input_grad_body(own, low, high, left, right, masked, maskb, kern, dx, dxm, wide):
    rows, cols = own.shape[1], own.shape[2]
    widen(wide, own, low, high, left, right)

    def emit(micro, first, chunk, lanes, total):
        at = slice(first, first + chunk)
        value = (total + masked[micro, at, :, lanes].astype(F32)).astype(BF16)
        dx[micro, at, :, lanes] = value
        dxm[micro, at, :, lanes] = (value.astype(F32) * maskb[at]).astype(BF16)

    depthwise(wide, kern, rows, cols, SIDE - HALO, True, emit)


def weight_grad_body(parts, carried, factor, *refs):
    normed, masked = refs[:parts], refs[parts : 2 * parts]
    w_in, b_in, w_out = refs[2 * parts : 2 * parts + 3]
    grad_in, grad_out, sum_in, sum_out = refs[-4:]
    if carried:
        sum_in[...] = refs[2 * parts + 3][...]
        sum_out[...] = refs[2 * parts + 4][...]
    else:
        sum_in[...] = jnp.zeros_like(sum_in)
        sum_out[...] = jnp.zeros_like(sum_out)
    for part in range(parts):
        cells = normed[part].shape[0]
        step = min(cells, 256)

        @pl.loop(0, cells // step)
        def _(index):
            at = pl.ds(pl.multiple_of(index * step, step), step)
            n = normed[part][at, :]
            gm = masked[part][at, :]
            h = jnp.dot(n, w_in[...], preferred_element_type=F32) + b_in[...]
            act, slope = gelu_both(h)
            dhid = (nt_dot(gm, w_out[...]) * slope).astype(BF16)
            sum_in[...] += tn_dot(n, dhid)
            sum_out[...] += tn_dot(act.astype(BF16), gm)

    grad_in[...] = sum_in[...] * factor
    grad_out[...] = sum_out[...] * factor


def lat_edges(first, last):
    count = lax.axis_size("lat")
    if count == 1:
        return jnp.zeros_like(last), jnp.zeros_like(first)
    if count == 2:
        index = lax.axis_index("lat")
        got = lax.ppermute(jnp.where(index == 0, last, first), "lat", [(0, 1), (1, 0)])
        none = jnp.zeros_like(got)
        return jnp.where(index == 0, none, got), jnp.where(index == 0, got, none)
    up = [(i, i + 1) for i in range(count - 1)]
    low = lax.ppermute(last, "lat", up)
    return low, lax.ppermute(first, "lat", [(b, a) for a, b in up])


def halo(own):
    low, high = lat_edges(own[:, :HALO], own[:, -HALO:])
    count = lax.axis_size("lon")
    firsts = jnp.concatenate([v[:, :, :HALO] for v in (low, own, high)], axis=1)
    lasts = jnp.concatenate([v[:, :, -HALO:] for v in (low, own, high)], axis=1)
    ring = [(i, (i + 1) % count) for i in range(count)]
    left = lax.ppermute(lasts, "lon", ring)
    right = lax.ppermute(firsts, "lon", [(b, a) for a, b in ring])
    return low, high, left, right


def ring_pieces(value, axis):
    count = lax.axis_size(axis)
    return [value] + [
        lax.ppermute(value, axis, [(i, (i + d) % count) for i in range(count)])
        for d in range(1, count)
    ]


def crossing_pieces(value):
    count = lax.axis_size("lon")
    pieces = []
    for d in range(count):
        pairs = []
        for i in range(count):
            for s in range(2):
                pairs.append((i * 2 + s, ((i + d) % count) * 2 + 1 - s))
        pieces.append(lax.ppermute(value, ("lon", "section"), pairs))
    return pieces


def summed(value):
    for axis in ("lat", "lon"):
        count = lax.axis_size(axis)
        if count & (count - 1):
            value = lax.psum(value, axis)
            continue
        step = 1
        while step < count:
            value = value + lax.ppermute(value, axis, [(i, i ^ step) for i in range(count)])
            step *= 2
    return value


def weight_grads(normed, masked, factor, w_in, b_in, w_out, carried=()):
    chans, hidden = w_in.shape
    return call(
        functools.partial(weight_grad_body, len(normed), bool(carried), factor),
        [like((chans, hidden), F32), like((hidden, chans), F32)],
        [pltpu.VMEM((chans, hidden), F32), pltpu.VMEM((hidden, chans), F32)],
        *normed, *masked, w_in, b_in, w_out, *carried,
        micros=sum(v.shape[0] for v in normed) / 200.0,
    )


def tile_shards(
    saved_inputs, out_cotangent, land_mask, conv_kernel, conv_bias, norm_gain, w_in, b_in, w_out
):
    micros, rows, cols, chans = out_cotangent.shape
    hidden = w_in.shape[2]
    cells = micros * rows * cols
    shape = (micros, rows, cols, chans)
    wide_shape = (micros, rows + 2 * HALO, SIDE + cols + SIDE, chans)
    flat = (cells, chans)
    tiles = lax.axis_size("lat") * lax.axis_size("lon")
    factor = 1.0 / (cells * tiles) ** 0.5
    section = lax.axis_index("section")
    gather = tiles <= GATHER_TILES

    kern = conv_kernel[0].reshape(49, chans).astype(F32)
    weight_in, weight_out = w_in[0], w_out[0]
    maskf = land_mask.astype(F32)
    maskb = jnp.broadcast_to(maskf[:, :, None], (rows, cols, LANES))
    masked1 = (out_cotangent.astype(F32) * maskf[None, :, :, None]).astype(BF16)

    x = saved_inputs[0]
    wide, normed, zhat, rscale, slope, dz = call(
        forward_body,
        [
            like(wide_shape, F32),
            like(flat, BF16),
            like(flat, F32),
            like((cells, 1), F32),
            like((cells, hidden), F32),
            like(flat, BF16),
        ],
        [pltpu.VMEM(flat, F32)],
        x, *halo(x), masked1.reshape(flat), kern, conv_bias, norm_gain, weight_in, b_in, weight_out,
        micros=3.0,
    )
    if gather:
        normed_row = jnp.concatenate(ring_pieces(normed, "lon"))
        normed_all = ring_pieces(normed_row, "lat")

    def input_grad(dz, masked):
        dz = dz.reshape(shape)
        edges = halo(dz)
        (grad_k,) = call(
            functools.partial(kernel_grad_body, SIDE - HALO),
            [like((49, chans), F32)],
            [],
            wide, dz,
            micros=3.0,
        )
        dx, dxm = call(
            input_grad_body,
            [like(shape, BF16), like(shape, BF16)],
            [pltpu.VMEM(wide_shape, F32)],
            dz, *edges, masked, maskb, kern,
            micros=3.0,
        )
        return grad_k, dx, dxm

    grad_k1, dx1, dxm1 = input_grad(dz, masked1)
    cross = jnp.where(section == 1, dxm1, masked1).reshape(flat)
    if gather:
        pieces = crossing_pieces(cross)
        masked0 = pieces[0]
        masked_all = ring_pieces(jnp.concatenate(pieces), "lat")
    else:
        masked0 = lax.ppermute(cross, "section", [(0, 1), (1, 0)])
        normed_all, masked_all = [normed], [masked0]
    (dz0,) = call(
        back_body, [like(flat, BF16)], [],
        masked0, slope, zhat, rscale, norm_gain, weight_in, weight_out,
        micros=3.0,
    )
    grad_k0, dx0, _ = input_grad(dz0, masked0.reshape(shape))
    grad_k = summed(jnp.where(section == 1, grad_k1, grad_k0)) * factor
    grad_in, grad_out = weight_grads(
        normed_all, masked_all, factor, weight_in, b_in, weight_out
    )
    if not gather:
        grad_in, grad_out = lax.psum((grad_in, grad_out), ("lon", "lat"))
    results = jnp.where(section == 1, dx1, dx0)
    return results[None], grad_in[None], grad_out[None], grad_k[None]


def copied(pairs, sems):
    copies = [pltpu.make_async_copy(a, b, sems.at[i]) for i, (a, b) in enumerate(pairs)]
    for copy in copies:
        copy.start()
    return copies


def prepare_body(
    place, x_far, g_far, mask_far, x, sent, near, far, g, mask, firsts, lasts, sems
):
    micros, rows, cols, chans = x.shape
    for copy in copied([(x_far, x), (g_far, g), (mask_far, mask)], sems):
        copy.wait()
    maskb = jnp.broadcast_to(mask[...].astype(F32)[:, :, None], (rows, cols, chans))
    gm = g[...].astype(F32) * maskb[None]
    sent[:micros] = gm.astype(BF16)
    sent[micros] = maskb.astype(BF16)
    xf = x[...].astype(F32)
    for row in range(micros * rows):
        micro, at = row // rows, row % rows
        for buf, x_cols, g_cols in (
            (firsts, slice(0, 2 * HALO), slice(0, HALO)),
            (lasts, slice(cols - 2 * HALO, cols), slice(cols - HALO, cols)),
        ):
            buf[row * 9 : row * 9 + 6, :] = xf[micro, at, x_cols]
            buf[row * 9 + 6 : row * 9 + 9, :] = gm[micro, at, g_cols]

    @pl.when(place[0] == 1)
    def _():
        near[...] = lasts[...].astype(BF16)
        far[...] = firsts[...].astype(BF16)

    @pl.when(place[0] == 0)
    def _():
        near[...] = firsts[...].astype(BF16)
        far[...] = lasts[...].astype(BF16)


def stage_body(near, masked, taps, *refs):
    count = (len(refs) - 4) // 2
    sources, kern, sent, targets = refs[:count], refs[count], refs[count + 1], refs[count + 2 : -2]
    held, sems = refs[-2:]
    copies = copied(list(zip(sources, targets)) + [(taps, held)], sems)
    sent[...] = masked[...]
    for copy in copies:
        copy.wait()
    for ka in range(7):
        kern[ka * 7 : ka * 7 + 7, :] = held[0, ka].astype(F32)


def norm_body(
    place, x, xp, near, far, kern, bias, gain, w_in, b_in,
    wide, normed, zhat, rscale, slope, zval, packed,
):
    micros, rows, cols, chans = x.shape
    half = cols // 2
    all_rows = 2 * rows
    reach = half + 8
    side, lat = place[0], place[1]
    wide[...] = jnp.zeros_like(wide)
    for tile, edge, at in ((x, near, lat * rows), (xp, far, (1 - lat) * rows)):
        own_rows = pl.ds(HALO + at, rows)
        tile_x = tile[...].astype(F32)
        packed[...] = edge[...].astype(F32)

        @pl.when(side == 0)
        def _():
            for row in range(micros * rows):
                micro, to = row // rows, row % rows
                wide[micro, at + HALO + to, : 2 * HALO, :] = packed[row * 9 : row * 9 + 6, :]
            wide[:, own_rows, 2 * HALO : 2 * HALO + cols, :] = tile_x

        @pl.when(side == 1)
        def _():
            skip = half - 2 * HALO
            wide[:, own_rows, : cols - skip, :] = tile_x[:, :, skip:]
            for row in range(micros * rows):
                micro, to = row // rows, row % rows
                wide[micro, at + HALO + to, cols - skip : cols - skip + 2 * HALO, :] = packed[
                    row * 9 : row * 9 + 6, :
                ]

    def emit(micro, first, chunk, lanes, total):
        at = (micro * all_rows + first) * reach
        zval[at : at + chunk * reach, lanes] = total.reshape(chunk * reach, LANES)

    depthwise(wide, kern, all_rows, reach, 0, False, emit)
    z = zval[...] + bias[...]
    centred = z - jnp.mean(z, axis=-1, keepdims=True)
    rs = lax.rsqrt(jnp.mean(centred * centred, axis=-1, keepdims=True) + 1e-06)
    zh = centred * rs
    zhat[...] = zh
    rscale[...] = rs
    n = zh * gain[...]
    core = n.reshape(micros * all_rows, reach, chans)[:, HALO : HALO + half]
    normed[...] = core.reshape(normed.shape).astype(BF16)
    h = jnp.dot(n.astype(BF16), w_in[...], preferred_element_type=F32) + b_in[...]
    slope[...] = gelu_both(h)[1]


def pair_back(gwide, dwide, zhat, rscale, slope, gain, w_in, w_out, kern, dz, emit):
    micros, rows, reach, chans = gwide.shape
    half = reach - 8
    masked = gwide[...].reshape(micros * rows * reach, chans).astype(BF16)
    dzval = dense_back(
        masked, slope[...], zhat[...], rscale[...], gain[...], w_in[...], w_out[...]
    )
    rounded = dzval.astype(BF16).astype(F32).reshape(micros, rows, reach, chans)
    nothing = jnp.zeros((micros, HALO, reach, chans), F32)
    dwide[:, :HALO] = nothing
    dwide[:, HALO + rows :] = nothing
    dwide[:, HALO : HALO + rows] = rounded
    dz[...] = rounded[:, :, HALO : HALO + half].astype(BF16)

    def add(micro, first, chunk, lanes, total):
        own = gwide[micro, first : first + chunk, HALO : HALO + half, lanes]
        emit(micro, slice(first, first + chunk), lanes, (total + own).astype(BF16))

    depthwise(dwide, kern, rows, half, 0, True, add)


def last_back_body(place, *refs):
    @pl.when(place[2] == 1)
    def _():
        last_back_work(place, *refs)


def last_back_work(
    place, gm, gmp, near, far, zhat, rscale, slope, gain, w_in, w_out, kern,
    dx, dxm, first3, last3, dz, core, gwide, dwide, mask, packed,
):
    micros, all_rows, half, chans = dx.shape
    rows, cols = all_rows // 2, 2 * half
    side, lat = place[0], place[1]
    gwide[:, :, half:, :] = jnp.zeros((micros, all_rows, 8, chans), F32)
    for tile, edge, at in ((gm, near, lat * rows), (gmp, far, (1 - lat) * rows)):
        to_rows = pl.ds(at, rows)
        both = tile[...].astype(F32)
        packed[...] = edge[...].astype(F32)

        @pl.when(side == 0)
        def _():
            gwide[:, to_rows, HALO : 2 * HALO + half, :] = both[:micros, :, : half + HALO]
            for row in range(micros * rows):
                gwide[row // rows, at + row % rows, :HALO, :] = packed[row * 9 + 6 : row * 9 + 9, :]
            mask[to_rows] = both[micros, :, :half]

        @pl.when(side == 1)
        def _():
            gwide[:, to_rows, : HALO + half, :] = both[:micros, :, half - HALO :]
            for row in range(micros * rows):
                gwide[row // rows, at + row % rows, HALO + half : 2 * HALO + half, :] = packed[
                    row * 9 + 6 : row * 9 + 9, :
                ]
            mask[to_rows] = both[micros, :, half:]

    core[...] = gwide[:, :, HALO : HALO + half, :].astype(BF16)

    def emit(micro, at, lanes, value):
        dx[micro, at, :, lanes] = value
        kept = value.astype(F32) * mask[at, :, lanes]
        dxm[micro, at, :, lanes] = kept.astype(BF16)
        first3[micro, at, :, lanes] = kept[:, :HALO].astype(BF16)
        last3[micro, at, :, lanes] = kept[:, half - HALO :].astype(BF16)

    pair_back(gwide, dwide, zhat, rscale, slope, gain, w_in, w_out, kern, dz, emit)


def first_back_body(place, *refs):
    @pl.when(place[2] == 0)
    def _():
        first_back_work(*refs)


def first_back_work(
    core, left, right, zhat, rscale, slope, gain, w_in, w_out, kern, dx, dz, gwide, dwide
):
    micros, rows, half, chans = core.shape
    gwide[:, :, half:, :] = jnp.zeros((micros, rows, 8, chans), F32)
    gwide[:, :, :HALO, :] = left[...].astype(F32)
    gwide[:, :, HALO : HALO + half, :] = core[...].astype(F32)
    gwide[:, :, HALO + half : 2 * HALO + half, :] = right[...].astype(F32)

    def emit(micro, at, lanes, value):
        dx[micro, at, :, lanes] = value

    pair_back(gwide, dwide, zhat, rscale, slope, gain, w_in, w_out, kern, dz, emit)


def pair_up(target, first, second):
    half = first.shape[0]
    target[:half] = first[...]
    target[half:] = second[...]


def edge_body(first3, normed, got, sent, pair):
    sent[...] = first3[...]
    pair_up(pair, normed, got)


def select_join_body(place, core1, got1, core0, got0, pair):
    half = pair.shape[0] // 2
    for number, core, got in ((1, core1, got1), (0, core0, got0)):

        @pl.when(place[2] == number)
        def _():
            pair[:half] = core[...].reshape(half, pair.shape[1])
            pair[half:] = got[...].reshape(half, pair.shape[1])


def pair_kernel_grad_body(place, wide, dz1, dz0, after, grad, dz):
    @pl.when(place[2] == 1)
    def _():
        dz[...] = dz1[...]

    @pl.when(place[2] == 0)
    def _():
        dz[...] = dz0[...]

    kernel_grad_body(HALO, wide, dz, grad)


def pair_shards(
    saved_inputs, out_cotangent, land_mask, conv_kernel, conv_bias, norm_gain, w_in, b_in, w_out
):
    micros, rows, cols, chans = out_cotangent.shape
    hidden = w_in.shape[2]
    lons = lax.axis_size("lon")
    half, all_rows, reach = cols // 2, 2 * rows, cols // 2 + 8
    cells = micros * all_rows * half
    many = micros * all_rows * reach
    shape = (micros, all_rows, half, chans)
    edge_shape = (micros, all_rows, HALO, chans)
    wide_shape = (micros, all_rows + 2 * HALO, reach + 8, chans)
    reach_shape = (micros, all_rows, reach, chans)
    factor = 1.0 / (cells * 2 * lons) ** 0.5
    section, lat, lon = (lax.axis_index(a) for a in ("section", "lat", "lon"))
    side = jnp.bitwise_xor(lat, jnp.bitwise_and(lon, 1))
    count = 2 * lons

    def device(position):
        position = position % count
        tile, which = position // 2, position % 2
        return tile * 2 + (which ^ (tile & 1))

    x = saved_inputs[0]
    place = jnp.stack([side, lat, section]).astype(jnp.int32)
    packed = (micros * rows * 3 * HALO, chans)
    sent_shape = (micros + 1, rows, cols, chans)

    swap = [(0, 1), (1, 0)]
    xp = lax.ppermute(x, "lat", swap)
    anywhere, vmem = pl.BlockSpec(memory_space=pl.ANY), pl.BlockSpec(memory_space=pltpu.VMEM)
    hbm, smem = pl.BlockSpec(memory_space=pltpu.HBM), pl.BlockSpec(memory_space=pltpu.SMEM)
    x_near, masked, near, far = call(
        prepare_body,
        [like(x.shape, BF16), like(sent_shape, BF16), like(packed, BF16), like(packed, BF16)],
        [
            pltpu.VMEM(x.shape, BF16),
            pltpu.VMEM(land_mask.shape, land_mask.dtype),
            pltpu.VMEM(packed, F32),
            pltpu.VMEM(packed, F32),
            pltpu.SemaphoreType.DMA((3,)),
        ],
        place, x, out_cotangent, land_mask,
        specs=[smem, hbm, hbm, hbm],
    )
    near_pairs = [(device(p), device(p + 1 if p % 2 else p - 1)) for p in range(count)]
    far_pairs = [(device(p), device(p - 2 if p % 2 else p + 2)) for p in range(count)]
    near = lax.ppermute(near, ("lon", "lat"), near_pairs)
    far = lax.ppermute(far, ("lon", "lat"), far_pairs)
    params = [conv_bias, norm_gain, w_in[0], b_in, w_out[0]]
    kern, masked, bias, gain, weight_in, bias_in, weight_out = call(
        stage_body,
        [like((49, chans), F32), like(sent_shape, BF16)] + [like(v.shape, v.dtype) for v in params],
        [pltpu.VMEM(conv_kernel.shape, BF16), pltpu.SemaphoreType.DMA((len(params) + 1,))],
        near, masked, conv_kernel, *params,
        specs=[anywhere, vmem] + [hbm] * (1 + len(params)),
    )
    gmp = lax.ppermute(masked, ("lat", "section"), [(1, 3), (3, 1)])

    wide, normed, zhat, rscale, slope = call(
        norm_body,
        [
            like(wide_shape, F32),
            like((cells, chans), BF16),
            like((many, chans), F32),
            like((many, 1), F32),
            like((many, hidden), F32),
        ],
        [pltpu.VMEM((many, chans), F32), pltpu.VMEM(packed, F32)],
        place, x_near, xp, near, far, kern, bias, gain, weight_in, bias_in,
        micros=6.5,
        scalars=1,
    )
    state = (zhat, rscale, slope, gain, weight_in, weight_out, kern)
    buffers = [
        pltpu.VMEM(reach_shape, F32),
        pltpu.VMEM((micros, all_rows + 2 * HALO, reach, chans), F32),
    ]
    dx1, dxm1, first3, last3, dz1, core1 = call(
        last_back_body,
        [like(shape, BF16), like(shape, BF16), like(edge_shape, BF16), like(edge_shape, BF16)]
        + [like(shape, BF16), like(shape, BF16)],
        buffers + [pltpu.VMEM(shape[1:], F32), pltpu.VMEM(packed, F32)],
        place, masked, gmp, near, far, *state,
        micros=4.5,
        scalars=1,
    )
    far_step = lons // 2

    def exchanged(value, axis, step):
        return lax.ppermute(value, axis, [(i, i ^ step) for i in range(lax.axis_size(axis))])

    def across(value, to):
        pairs = [(i * 2 + 1, (i ^ far_step) * 2 + to) for i in range(lons)]
        return lax.ppermute(value, ("lon", "section"), pairs)

    axes = ("lon", "lat", "section")
    core0 = lax.ppermute(dxm1, "section", [(1, 0)])
    left0 = lax.ppermute(
        last3, axes, [(device(p) * 2 + 1, device(p + 1) * 2) for p in range(count)]
    )
    first3, normed_pair = call(
        edge_body,
        [like(edge_shape, BF16), like((2 * cells, chans), BF16)],
        [],
        first3, normed, exchanged(normed, "lon", far_step),
        micros=0.5,
    )
    right0 = lax.ppermute(
        first3, axes, [(device(p) * 2 + 1, device(p - 1) * 2) for p in range(count)]
    )
    (masked_pair,) = call(
        select_join_body,
        [like((2 * cells, chans), BF16)],
        [],
        place, core1, across(core1, 1), core0, across(dxm1, 0),
        micros=0.5,
        scalars=1,
    )
    dx0, dz0 = call(
        first_back_body,
        [like(shape, BF16), like(shape, BF16)],
        buffers,
        place, core0, left0, right0, *state,
        micros=4.5,
        scalars=1,
    )
    parts = [(normed_pair, masked_pair)]
    if lons == 4:
        parts.append((exchanged(normed_pair, "lon", 1), exchanged(masked_pair, "lon", 1)))
    parts += [tuple(lax.ppermute(v, "lat", swap) for v in part) for part in parts]

    (grad_k,) = call(
        pair_kernel_grad_body,
        [like((49, chans), F32)],
        [pltpu.VMEM(shape, BF16)],
        place, wide, dz1, dz0, parts[1][1],
        micros=3.0,
        specs=[smem] + [vmem] * 3 + [anywhere],
    )
    grad_k = summed(grad_k) * factor
    sums = ()
    for index, part in enumerate(parts):
        scale = factor if index == len(parts) - 1 else 1.0
        sums = weight_grads(
            [part[0]], [part[1]], scale, weight_in, bias_in, weight_out, sums
        )
    grad_in, grad_out = sums

    result = jnp.where(section == 1, dx1, dx0)
    kept = lax.dynamic_slice_in_dim(result, lat * rows, rows, 1)
    given = lax.dynamic_slice_in_dim(result, (1 - lat) * rows, rows, 1)
    got = lax.ppermute(given, "lat", swap)
    low = jnp.where(side == 0, kept, got)
    high = jnp.where(side == 0, got, kept)
    result = jnp.concatenate([low, high], axis=2)
    return result[None], grad_in[None], grad_out[None], grad_k[None]


def shards(saved_inputs, out_cotangent, *rest):
    lats, lons = lax.axis_size("lat"), lax.axis_size("lon")
    paired = lats == 2 and lons in (2, 4) and lats * lons <= GATHER_TILES
    rows, cols = out_cotangent.shape[1:3]
    paired = paired and rows % 8 == 0 and cols == 16
    body = pair_shards if paired else tile_shards
    return body(saved_inputs, out_cotangent, *rest)


def solution(mesh):
    in_specs = (
        P("section", "group", "lat", "lon", None),
        P("group", "lat", "lon", None),
        P("lat", "lon"),
        P("section", None, None, None),
        P("section", None),
        P("section", None),
        P("section", None, None),
        P("section", None),
        P("section", None, None),
    )
    out_specs = (
        P("section", "group", "lat", "lon", None),
        P("section", "group", None),
        P("section", "group", None),
        P("section", "group", None),
    )
    return jax.shard_map(shards, mesh=mesh, in_specs=in_specs, out_specs=out_specs, check_vma=False)
```

```python
import functools
import jax
import jax.numpy as jnp
from jax import lax
from jax.experimental import pallas as pl
from jax.experimental.pallas import tpu as pltpu
from jax.sharding import PartitionSpec as P

gelu_k = 0.7978845608028654
gelu_c = 0.044715
LANES = 128
HALO = 3
SIDE = 8
F32 = jnp.float32
BF16 = jnp.bfloat16
VMEM_LIMIT = 16 * 1024 * 1024
GATHER_TILES = 8


def call(body, outs, scratch, *args, micros=1.0, scalars=0, specs=None, limit=VMEM_LIMIT):
    if specs is None:
        specs = [pl.BlockSpec(memory_space=pltpu.SMEM)] * scalars
        specs += [pl.BlockSpec(memory_space=pltpu.VMEM)] * (len(args) - scalars)
    return pl.pallas_call(
        body,
        out_shape=outs,
        in_specs=specs,
        out_specs=[pl.BlockSpec(memory_space=pltpu.VMEM)] * len(outs),
        scratch_shapes=scratch,
        compiler_params=pltpu.CompilerParams(vmem_limit_bytes=limit),
        cost_estimate=pl.CostEstimate(
            flops=int(micros * 1.1e9), bytes_accessed=int(micros * 3.6e6), transcendentals=0
        ),
    )(*args)


def like(shape, dtype):
    return jax.ShapeDtypeStruct(shape, dtype)


def nt_dot(left, right):
    return lax.dot_general(left, right, (((1,), (1,)), ((), ())), preferred_element_type=F32)


def tn_dot(left, right):
    return lax.dot_general(left, right, (((0,), (0,)), ((), ())), preferred_element_type=F32)


def gelu_both(h):
    k, c, c3, half, one = (
        jnp.asarray(v, h.dtype) for v in (gelu_k, gelu_k * gelu_c, 3.0 * gelu_k * gelu_c, 0.5, 1.0)
    )
    h2 = h * h
    tval = jnp.tanh(h * (k + c * h2))
    rise = half + half * tval
    return h * rise, rise + (half * h) * (one - tval * tval) * (k + c3 * h2)


def lane_parts(chans):
    return [slice(at, at + LANES) for at in range(0, chans, LANES)]


def widen(dst, own, low, high, left, right):
    rows, cols = own.shape[1], own.shape[2]
    for part, lanes in enumerate(lane_parts(own.shape[3])):
        to = dst.at[part]
        to[:, :HALO, SIDE : SIDE + cols, :] = low[:, :, :, lanes].astype(F32)
        to[:, HALO : HALO + rows, SIDE : SIDE + cols, :] = own[:, :, :, lanes].astype(F32)
        to[:, HALO + rows :, SIDE : SIDE + cols, :] = high[:, :, :, lanes].astype(F32)
        to[:, :, SIDE - HALO : SIDE, :] = left[:, :, :, lanes].astype(F32)
        to[:, :, SIDE + cols : SIDE + cols + HALO, :] = right[:, :, :, lanes].astype(F32)


def depthwise(src, kern, rows, cols, begin, flip, emit):
    chunk = 8 if cols > 8 else 16
    chunk = chunk if rows % chunk == 0 else rows
    for part, lanes in enumerate(lane_parts(kern.shape[1])):
        for micro in range(src.shape[1]):
            for first in range(0, rows, chunk):
                total = jnp.zeros((chunk, cols, LANES), F32)
                for kb in range(7):
                    at = slice(begin + kb, begin + kb + cols)
                    slab = src[part, micro, first : first + chunk + 2 * HALO, at, :]
                    for ka in range(7):
                        tap = (6 - ka) * 7 + (6 - kb) if flip else ka * 7 + kb
                        total = total + slab[ka : ka + chunk] * kern[tap : tap + 1, lanes]
                emit(micro, first, chunk, lanes, total)


def dense_back(masked, slope, zhat, rscale, gain, w_in, w_out):
    dact = nt_dot(masked, w_out)
    dhid = (dact * slope).astype(BF16)
    dzh = nt_dot(dhid, w_in) * gain
    return rscale * (
        dzh
        - jnp.mean(dzh, axis=-1, keepdims=True)
        - zhat * jnp.mean(dzh * zhat, axis=-1, keepdims=True)
    )


def forward_body(
    x, low, high, left, right, masked, kern, bias, gain, w_in, b_in, w_out,
    wide, normed, zhat, rscale, slope, dz, zval,
):
    rows, cols = x.shape[1], x.shape[2]
    widen(wide, x, low, high, left, right)

    def emit(micro, first, chunk, lanes, total):
        at = (micro * rows + first) * cols
        zval[at : at + chunk * cols, lanes] = total.reshape(chunk * cols, LANES)

    depthwise(wide, kern, rows, cols, SIDE - HALO, False, emit)
    z = zval[...] + bias[...]
    centred = z - jnp.mean(z, axis=-1, keepdims=True)
    rs = lax.rsqrt(jnp.mean(centred * centred, axis=-1, keepdims=True) + 1e-06)
    zh = centred * rs
    n = (zh * gain[...]).astype(BF16)
    normed[...] = n
    zhat[...] = zh
    rscale[...] = rs
    h = jnp.dot(n, w_in[...], preferred_element_type=F32) + b_in[...]
    _, sl = gelu_both(h)
    slope[...] = sl
    dz[...] = dense_back(masked[...], sl, zh, rs, gain[...], w_in[...], w_out[...]).astype(BF16)


def back_body(masked, slope, zhat, rscale, gain, w_in, w_out, dz):
    dz[...] = dense_back(
        masked[...], slope[...], zhat[...], rscale[...], gain[...], w_in[...], w_out[...]
    ).astype(BF16)


def kernel_grad_body(first, wide, dz, grad):
    micros, rows, cols, chans = dz.shape
    for part, lanes in enumerate(lane_parts(chans)):
        for kb in range(7):
            begin = first + kb
            sums = [None] * 7
            for micro in range(micros):
                own = dz[micro, :, :, lanes].astype(F32)
                slab = wide[part, micro, :, begin : begin + cols, :]
                for ka in range(7):
                    prod = jnp.sum(slab[ka : ka + rows] * own, axis=0)
                    sums[ka] = prod if sums[ka] is None else sums[ka] + prod
            for ka in range(7):
                tap = ka * 7 + kb
                grad[tap : tap + 1, lanes] = jnp.sum(sums[ka], axis=0, keepdims=True)


def input_grad_body(own, low, high, left, right, masked, maskb, kern, dx, dxm, wide):
    rows, cols = own.shape[1], own.shape[2]
    widen(wide, own, low, high, left, right)

    def emit(micro, first, chunk, lanes, total):
        at = slice(first, first + chunk)
        value = (total + masked[micro, at, :, lanes].astype(F32)).astype(BF16)
        dx[micro, at, :, lanes] = value
        dxm[micro, at, :, lanes] = (value.astype(F32) * maskb[at]).astype(BF16)

    depthwise(wide, kern, rows, cols, SIDE - HALO, True, emit)


def weight_grad_body(parts, carried, factor, *refs):
    normed, masked = refs[:parts], refs[parts : 2 * parts]
    w_in, b_in, w_out = refs[2 * parts : 2 * parts + 3]
    grad_in, grad_out, token, sum_in, sum_out = refs[-5:]
    if carried:
        sum_in[...] = refs[2 * parts + 3][...]
        sum_out[...] = refs[2 * parts + 4][...]
    else:
        sum_in[...] = jnp.zeros_like(sum_in)
        sum_out[...] = jnp.zeros_like(sum_out)
    for part in range(parts):
        cells = normed[part].shape[0]
        step = min(cells, 512)

        @pl.loop(0, cells // step)
        def _(index):
            at = pl.ds(pl.multiple_of(index * step, step), step)
            n = normed[part][at, :]
            gm = masked[part][at, :]
            h = jnp.dot(n, w_in[...], preferred_element_type=F32) + b_in[...]
            act, slope = gelu_both(h.astype(BF16))
            dhid = nt_dot(gm, w_out[...]).astype(BF16) * slope
            sum_in[...] += tn_dot(n, dhid)
            sum_out[...] += tn_dot(act, gm)

    grad_in[...] = sum_in[...] * factor
    grad_out[...] = sum_out[...] * factor
    token[...] = jnp.zeros_like(token)


def lat_edges(first, last):
    count = lax.axis_size("lat")
    if count == 1:
        return jnp.zeros_like(last), jnp.zeros_like(first)
    if count == 2:
        index = lax.axis_index("lat")
        got = lax.ppermute(jnp.where(index == 0, last, first), "lat", [(0, 1), (1, 0)])
        none = jnp.zeros_like(got)
        return jnp.where(index == 0, none, got), jnp.where(index == 0, got, none)
    up = [(i, i + 1) for i in range(count - 1)]
    low = lax.ppermute(last, "lat", up)
    return low, lax.ppermute(first, "lat", [(b, a) for a, b in up])


def halo(own):
    low, high = lat_edges(own[:, :HALO], own[:, -HALO:])
    count = lax.axis_size("lon")
    firsts = jnp.concatenate([v[:, :, :HALO] for v in (low, own, high)], axis=1)
    lasts = jnp.concatenate([v[:, :, -HALO:] for v in (low, own, high)], axis=1)
    ring = [(i, (i + 1) % count) for i in range(count)]
    left = lax.ppermute(lasts, "lon", ring)
    right = lax.ppermute(firsts, "lon", [(b, a) for a, b in ring])
    return low, high, left, right


def ring_pieces(value, axis):
    count = lax.axis_size(axis)
    return [value] + [
        lax.ppermute(value, axis, [(i, (i + d) % count) for i in range(count)])
        for d in range(1, count)
    ]


def crossing_pieces(value):
    count = lax.axis_size("lon")
    pieces = []
    for d in range(count):
        pairs = []
        for i in range(count):
            for s in range(2):
                pairs.append((i * 2 + s, ((i + d) % count) * 2 + 1 - s))
        pieces.append(lax.ppermute(value, ("lon", "section"), pairs))
    return pieces


def summed(value):
    for axis in ("lat", "lon"):
        count = lax.axis_size(axis)
        if count & (count - 1):
            value = lax.psum(value, axis)
            continue
        step = 1
        while step < count:
            value = value + lax.ppermute(value, axis, [(i, i ^ step) for i in range(count)])
            step *= 2
    return value


def weight_grads(normed, masked, factor, w_in, b_in, w_out, carried=(), after=()):
    chans, hidden = w_in.shape
    args = [*normed, *masked, w_in, b_in, w_out, *carried]
    specs = [pl.BlockSpec(memory_space=pltpu.VMEM)] * len(args)
    return call(
        functools.partial(weight_grad_body, len(normed), bool(carried), factor),
        [like((chans, hidden), F32), like((hidden, chans), F32), like((8, LANES), F32)],
        [pltpu.VMEM((chans, hidden), F32), pltpu.VMEM((hidden, chans), F32)],
        *args, *after,
        micros=0.6,
        specs=specs + [pl.BlockSpec(memory_space=pl.ANY)] * len(after),
    )


def tile_shards(
    saved_inputs, out_cotangent, land_mask, conv_kernel, conv_bias, norm_gain, w_in, b_in, w_out
):
    micros, rows, cols, chans = out_cotangent.shape
    hidden = w_in.shape[2]
    cells = micros * rows * cols
    shape = (micros, rows, cols, chans)
    wide_shape = (chans // LANES, micros, rows + 2 * HALO, SIDE + cols + SIDE, LANES)
    flat = (cells, chans)
    tiles = lax.axis_size("lat") * lax.axis_size("lon")
    factor = 1.0 / (cells * tiles) ** 0.5
    section = lax.axis_index("section")
    gather = tiles <= GATHER_TILES

    kern = conv_kernel[0].reshape(49, chans).astype(F32)
    weight_in, weight_out = w_in[0], w_out[0]
    maskf = land_mask.astype(F32)
    maskb = jnp.broadcast_to(maskf[:, :, None], (rows, cols, LANES))
    masked1 = (out_cotangent.astype(F32) * maskf[None, :, :, None]).astype(BF16)

    x = saved_inputs[0]
    wide, normed, zhat, rscale, slope, dz = call(
        forward_body,
        [
            like(wide_shape, F32),
            like(flat, BF16),
            like(flat, F32),
            like((cells, 1), F32),
            like((cells, hidden), F32),
            like(flat, BF16),
        ],
        [pltpu.VMEM(flat, F32)],
        x, *halo(x), masked1.reshape(flat), kern, conv_bias, norm_gain, weight_in, b_in, weight_out,
        micros=3.0,
    )
    if gather:
        normed_row = jnp.concatenate(ring_pieces(normed, "lon"))
        normed_all = ring_pieces(normed_row, "lat")

    def input_grad(dz, masked):
        dz = dz.reshape(shape)
        edges = halo(dz)
        (grad_k,) = call(
            functools.partial(kernel_grad_body, SIDE - HALO),
            [like((49, chans), F32)],
            [],
            wide, dz,
            micros=3.0,
        )
        dx, dxm = call(
            input_grad_body,
            [like(shape, BF16), like(shape, BF16)],
            [pltpu.VMEM(wide_shape, F32)],
            dz, *edges, masked, maskb, kern,
            micros=3.0,
        )
        return grad_k, dx, dxm

    grad_k1, dx1, dxm1 = input_grad(dz, masked1)
    cross = jnp.where(section == 1, dxm1, masked1).reshape(flat)
    if gather:
        pieces = crossing_pieces(cross)
        masked0 = pieces[0]
        masked_all = ring_pieces(jnp.concatenate(pieces), "lat")
    else:
        masked0 = lax.ppermute(cross, "section", [(0, 1), (1, 0)])
        normed_all, masked_all = [normed], [masked0]
    (dz0,) = call(
        back_body, [like(flat, BF16)], [],
        masked0, slope, zhat, rscale, norm_gain, weight_in, weight_out,
        micros=3.0,
    )
    grad_k0, dx0, _ = input_grad(dz0, masked0.reshape(shape))
    grad_k = summed(jnp.where(section == 1, grad_k1, grad_k0)) * factor
    grad_in, grad_out, _ = weight_grads(
        normed_all, masked_all, factor, weight_in, b_in, weight_out
    )
    if not gather:
        grad_in, grad_out = lax.psum((grad_in, grad_out), ("lon", "lat"))
    results = jnp.where(section == 1, dx1, dx0)
    return results[None], grad_in[None], grad_out[None], grad_k[None]


def copied(pairs, sems):
    copies = [pltpu.make_async_copy(a, b, sems.at[i]) for i, (a, b) in enumerate(pairs)]
    for copy in copies:
        copy.start()
    return copies


def prepare_body(
    place, x_far, g_far, mask_far, x, sent, near, far, g, mask, firsts, lasts, sems
):
    micros, rows, cols, chans = x.shape
    for copy in copied([(x_far, x), (g_far, g), (mask_far, mask)], sems):
        copy.wait()
    maskb = jnp.broadcast_to(mask[...].astype(F32)[:, :, None], (rows, cols, chans))
    gm = g[...].astype(F32) * maskb[None]
    sent[:micros] = gm.astype(BF16)
    sent[micros] = maskb.astype(BF16)
    xf = x[...].astype(F32)
    for row in range(micros * rows):
        micro, at = row // rows, row % rows
        for buf, x_cols, g_cols in (
            (firsts, slice(0, 2 * HALO), slice(0, HALO)),
            (lasts, slice(cols - 2 * HALO, cols), slice(cols - HALO, cols)),
        ):
            buf[row * 9 : row * 9 + 6, :] = xf[micro, at, x_cols]
            buf[row * 9 + 6 : row * 9 + 9, :] = gm[micro, at, g_cols]

    @pl.when(place[0] == 1)
    def _():
        near[...] = lasts[...].astype(BF16)
        far[...] = firsts[...].astype(BF16)

    @pl.when(place[0] == 0)
    def _():
        near[...] = firsts[...].astype(BF16)
        far[...] = lasts[...].astype(BF16)


def stage_body(near, masked, taps, *refs):
    count = (len(refs) - 4) // 2
    sources, kern, sent, targets = refs[:count], refs[count], refs[count + 1], refs[count + 2 : -2]
    held, sems = refs[-2:]
    copies = copied(list(zip(sources, targets)) + [(taps, held)], sems)
    sent[...] = masked[...]
    for copy in copies:
        copy.wait()
    for ka in range(7):
        kern[ka * 7 : ka * 7 + 7, :] = held[0, ka].astype(F32)


def norm_body(
    place, x, xp, near, far, kern, bias, gain, w_in, b_in,
    wide, normed, zhat, rscale, slope, zval, packed,
):
    micros, rows, cols, chans = x.shape
    half = cols // 2
    all_rows = 2 * rows
    reach = half + 8
    side, lat = place[0], place[1]
    wide[...] = jnp.zeros_like(wide)
    for tile, edge, at in ((x, near, lat * rows), (xp, far, (1 - lat) * rows)):
        own_rows = pl.ds(HALO + at, rows)
        tile_x = tile[...].astype(F32)
        packed[...] = edge[...].astype(F32)
        skip = half - 2 * HALO
        for number, keep, tile_at, edge_at in ((0, 0, 2 * HALO, 0), (1, skip, 0, cols - skip)):

            @pl.when(side == number)
            def _():
                for part, lanes in enumerate(lane_parts(chans)):
                    to_cols = slice(tile_at, tile_at + cols - keep)
                    wide[part, :, own_rows, to_cols, :] = tile_x[:, :, keep:, lanes]
                    for row in range(micros * rows):
                        wide[
                            part, row // rows, at + HALO + row % rows, edge_at : edge_at + 6, :
                        ] = packed[row * 9 : row * 9 + 6, lanes]

    def emit(micro, first, chunk, lanes, total):
        at = (micro * all_rows + first) * reach
        zval[at : at + chunk * reach, lanes] = total.reshape(chunk * reach, LANES)

    depthwise(wide, kern, all_rows, reach, 0, False, emit)
    z = zval[...] + bias[...]
    centred = z - jnp.mean(z, axis=-1, keepdims=True)
    rs = lax.rsqrt(jnp.mean(centred * centred, axis=-1, keepdims=True) + 1e-06)
    zh = centred * rs
    zhat[...] = zh
    rscale[...] = rs
    n = zh * gain[...]
    core = n.reshape(micros * all_rows, reach, chans)[:, HALO : HALO + half]
    normed[...] = core.reshape(normed.shape).astype(BF16)
    h = jnp.dot(n.astype(BF16), w_in[...], preferred_element_type=F32) + b_in[...]
    slope[...] = gelu_both(h)[1].astype(BF16)


def pair_back(gwide, dwide, zhat, rscale, slope, gain, w_in, w_out, kern, dz, emit):
    micros, rows, reach, chans = gwide.shape
    half = reach - 8
    masked = gwide[...].reshape(micros * rows * reach, chans).astype(BF16)
    dzval = dense_back(
        masked, slope[...].astype(F32), zhat[...], rscale[...], gain[...], w_in[...], w_out[...]
    )
    rounded = dzval.astype(BF16).astype(F32).reshape(micros, rows, reach, chans)
    nothing = jnp.zeros((micros, HALO, reach, LANES), F32)
    for part, lanes in enumerate(lane_parts(chans)):
        dwide[part, :, :HALO] = nothing
        dwide[part, :, HALO + rows :] = nothing
        dwide[part, :, HALO : HALO + rows] = rounded[..., lanes]
    dz[...] = rounded[:, :, HALO : HALO + half].astype(BF16)

    def add(micro, first, chunk, lanes, total):
        own = gwide[micro, first : first + chunk, HALO : HALO + half, lanes]
        emit(micro, slice(first, first + chunk), lanes, (total + own).astype(BF16))

    depthwise(dwide, kern, rows, half, 0, True, add)


def last_back_body(place, *refs):
    @pl.when(place[2] == 1)
    def _():
        last_back_work(place, *refs)


def last_back_work(
    place, gm, gmp, near, far, zhat, rscale, slope, gain, w_in, w_out, kern,
    dx, dxm, first3, last3, dz, core, gwide, dwide, mask, packed,
):
    micros, all_rows, half, chans = dx.shape
    rows, cols = all_rows // 2, 2 * half
    side, lat = place[0], place[1]
    gwide[:, :, half:, :] = jnp.zeros((micros, all_rows, 8, chans), F32)
    for tile, edge, at in ((gm, near, lat * rows), (gmp, far, (1 - lat) * rows)):
        to_rows = pl.ds(at, rows)
        both = tile[...].astype(F32)
        packed[...] = edge[...].astype(F32)

        @pl.when(side == 0)
        def _():
            gwide[:, to_rows, HALO : 2 * HALO + half, :] = both[:micros, :, : half + HALO]
            for row in range(micros * rows):
                gwide[row // rows, at + row % rows, :HALO, :] = packed[row * 9 + 6 : row * 9 + 9, :]
            mask[to_rows] = both[micros, :, :half]

        @pl.when(side == 1)
        def _():
            gwide[:, to_rows, : HALO + half, :] = both[:micros, :, half - HALO :]
            for row in range(micros * rows):
                gwide[row // rows, at + row % rows, HALO + half : 2 * HALO + half, :] = packed[
                    row * 9 + 6 : row * 9 + 9, :
                ]
            mask[to_rows] = both[micros, :, half:]

    core[...] = gwide[:, :, HALO : HALO + half, :].astype(BF16)

    def emit(micro, at, lanes, value):
        dx[micro, at, :, lanes] = value
        kept = value.astype(F32) * mask[at, :, lanes]
        dxm[micro, at, :, lanes] = kept.astype(BF16)
        first3[micro, at, :, lanes] = kept[:, :HALO].astype(BF16)
        last3[micro, at, :, lanes] = kept[:, half - HALO :].astype(BF16)

    pair_back(gwide, dwide, zhat, rscale, slope, gain, w_in, w_out, kern, dz, emit)


def first_back_body(place, *refs):
    @pl.when(place[2] == 0)
    def _():
        first_back_work(*refs)


def first_back_work(
    core, left, right, zhat, rscale, slope, gain, w_in, w_out, kern, dx, dz, gwide, dwide
):
    micros, rows, half, chans = core.shape
    gwide[:, :, half:, :] = jnp.zeros((micros, rows, 8, chans), F32)
    gwide[:, :, :HALO, :] = left[...].astype(F32)
    gwide[:, :, HALO : HALO + half, :] = core[...].astype(F32)
    gwide[:, :, HALO + half : 2 * HALO + half, :] = right[...].astype(F32)

    def emit(micro, at, lanes, value):
        dx[micro, at, :, lanes] = value

    pair_back(gwide, dwide, zhat, rscale, slope, gain, w_in, w_out, kern, dz, emit)


def pair_up(target, first, second):
    half = first.shape[0]
    target[:half] = first[...]
    target[half:] = second[...]


def pair_body(first, second, left0, right0, pair):
    pair_up(pair, first, second)


def select_join_body(place, core1, got1, core0, got0, left0, right0, pair):
    half = pair.shape[0] // 2
    for number, core, got in ((1, core1, got1), (0, core0, got0)):

        @pl.when(place[2] == number)
        def _():
            pair[:half] = core[...].reshape(half, pair.shape[1])
            pair[half:] = got[...].reshape(half, pair.shape[1])


def add_body(scale, first, second, after, out):
    total = (first[...] + second[...]) * scale
    if len(out.shape) == 2:
        out[...] = total
    else:
        for row in range(out.shape[0]):
            out[row] = total[row : row + 1]


def pair_kernel_grad_body(place, wide, dz1, dz0, after, grad, dz):
    for number, own in ((1, dz1), (0, dz0)):

        @pl.when(place[2] == number)
        def _():
            dz[...] = own[...]

    kernel_grad_body(HALO, wide, dz, grad)


def pair_shards(
    saved_inputs, out_cotangent, land_mask, conv_kernel, conv_bias, norm_gain, w_in, b_in, w_out
):
    micros, rows, cols, chans = out_cotangent.shape
    hidden = w_in.shape[2]
    lons = lax.axis_size("lon")
    half, all_rows, reach = cols // 2, 2 * rows, cols // 2 + 8
    cells = micros * all_rows * half
    many = micros * all_rows * reach
    shape = (micros, all_rows, half, chans)
    edge_shape = (micros, all_rows, HALO, chans)
    wide_shape = (chans // LANES, micros, all_rows + 2 * HALO, reach + 8, LANES)
    reach_shape = (micros, all_rows, reach, chans)
    factor = 1.0 / (cells * 2 * lons) ** 0.5
    section, lat, lon = (lax.axis_index(a) for a in ("section", "lat", "lon"))
    side = jnp.bitwise_xor(lat, jnp.bitwise_and(lon, 1))
    count = 2 * lons

    def device(position):
        position = position % count
        tile, which = position // 2, position % 2
        return tile * 2 + (which ^ (tile & 1))

    x = saved_inputs[0]
    place = jnp.stack([side, lat, section]).astype(jnp.int32)
    packed = (micros * rows * 3 * HALO, chans)
    sent_shape = (micros + 1, rows, cols, chans)

    swap = [(0, 1), (1, 0)]
    xp = lax.ppermute(x, "lat", swap)
    anywhere, vmem = pl.BlockSpec(memory_space=pl.ANY), pl.BlockSpec(memory_space=pltpu.VMEM)
    hbm, smem = pl.BlockSpec(memory_space=pltpu.HBM), pl.BlockSpec(memory_space=pltpu.SMEM)
    x_near, masked, near, far = call(
        prepare_body,
        [like(x.shape, BF16), like(sent_shape, BF16), like(packed, BF16), like(packed, BF16)],
        [
            pltpu.VMEM(x.shape, BF16),
            pltpu.VMEM(land_mask.shape, land_mask.dtype),
            pltpu.VMEM(packed, F32),
            pltpu.VMEM(packed, F32),
            pltpu.SemaphoreType.DMA((3,)),
        ],
        place, x, out_cotangent, land_mask,
        specs=[smem, hbm, hbm, hbm],
    )
    near_pairs = [(device(p), device(p + 1 if p % 2 else p - 1)) for p in range(count)]
    far_pairs = [(device(p), device(p - 2 if p % 2 else p + 2)) for p in range(count)]
    near = lax.ppermute(near, ("lon", "lat"), near_pairs)
    far = lax.ppermute(far, ("lon", "lat"), far_pairs)
    params = [conv_bias, norm_gain, w_in[0], b_in, w_out[0]]
    kern, masked, bias, gain, weight_in, bias_in, weight_out = call(
        stage_body,
        [like((49, chans), F32), like(sent_shape, BF16)] + [like(v.shape, v.dtype) for v in params],
        [pltpu.VMEM(conv_kernel.shape, BF16), pltpu.SemaphoreType.DMA((len(params) + 1,))],
        near, masked, conv_kernel, *params,
        specs=[anywhere, vmem] + [hbm] * (1 + len(params)),
    )
    gmp = lax.ppermute(masked, ("lat", "section"), [(1, 3), (3, 1)])

    wide, normed, zhat, rscale, slope = call(
        norm_body,
        [
            like(wide_shape, F32),
            like((cells, chans), BF16),
            like((many, chans), F32),
            like((many, 1), F32),
            like((many, hidden), BF16),
        ],
        [pltpu.VMEM((many, chans), F32), pltpu.VMEM(packed, F32)],
        place, x_near, xp, near, far, kern, bias, gain, weight_in, bias_in,
        micros=6.5,
        scalars=1,
    )
    state = (zhat, rscale, slope, gain, weight_in, weight_out, kern)
    buffers = [
        pltpu.VMEM(reach_shape, F32),
        pltpu.VMEM((chans // LANES, micros, all_rows + 2 * HALO, reach, LANES), F32),
    ]
    dx1, dxm1, first3, last3, dz1, core1 = call(
        last_back_body,
        [like(shape, BF16), like(shape, BF16), like(edge_shape, BF16), like(edge_shape, BF16)]
        + [like(shape, BF16), like(shape, BF16)],
        buffers + [pltpu.VMEM(shape[1:], F32), pltpu.VMEM(packed, F32)],
        place, masked, gmp, near, far, *state,
        micros=4.5,
        scalars=1,
    )
    far_step = lons // 2

    def exchanged(value, axis, step):
        return lax.ppermute(value, axis, [(i, i ^ step) for i in range(lax.axis_size(axis))])

    def across(value, to):
        pairs = [(i * 2 + 1, (i ^ far_step) * 2 + to) for i in range(lons)]
        return lax.ppermute(value, ("lon", "section"), pairs)

    axes = ("lon", "lat", "section")
    core0 = lax.ppermute(dxm1, "section", [(1, 0)])
    left0 = lax.ppermute(
        last3, axes, [(device(p) * 2 + 1, device(p + 1) * 2) for p in range(count)]
    )
    right0 = lax.ppermute(
        first3, axes, [(device(p) * 2 + 1, device(p - 1) * 2) for p in range(count)]
    )
    (masked_pair,) = call(
        select_join_body,
        [like((2 * cells, chans), BF16)],
        [],
        place, core1, across(core1, 1), core0, across(dxm1, 0), left0, right0,
        micros=0.5,
        specs=[smem] + [vmem] * 4 + [anywhere] * 2,
    )
    (normed_pair,) = call(
        pair_body,
        [like((2 * cells, chans), BF16)],
        [],
        normed, exchanged(normed, "lon", far_step), left0, right0,
        micros=0.5,
        specs=[vmem] * 2 + [anywhere] * 2,
    )
    dx0, dz0 = call(
        first_back_body,
        [like(shape, BF16), like(shape, BF16)],
        buffers,
        place, core0, left0, right0, *state,
        micros=4.5,
        scalars=1,
    )
    normed_near, masked_near = exchanged(normed_pair, "lon", 1), exchanged(masked_pair, "lon", 1)
    normed_far, masked_far = (lax.ppermute(v, "lat", swap) for v in (normed_pair, masked_pair))
    normed_last = exchanged(normed_far, "lon", 1)
    masked_last = lax.ppermute(masked_near, "lat", swap)

    (grad_k,) = call(
        pair_kernel_grad_body,
        [like((49, chans), F32)],
        [pltpu.VMEM(shape, BF16)],
        place, wide, dz1, dz0, normed_near,
        micros=3.0,
        specs=[smem] + [vmem] * 3 + [anywhere],
    )
    weights = (weight_in, bias_in, weight_out)

    def added(grad, axis, step, scale, shape, after):
        return call(
            functools.partial(add_body, scale),
            [like(shape, F32)],
            [],
            grad, exchanged(grad, axis, step), after,
            micros=0.2,
            specs=[vmem, vmem, anywhere],
        )[0]

    taps = grad_k.shape
    *sums, done = weight_grads([normed_pair], [masked_pair], 1.0, *weights)
    grad_k = added(grad_k, "lon", far_step, 1.0, taps, done)
    *sums, done = weight_grads([normed_near], [masked_near], 1.0, *weights, sums)
    grad_k = added(grad_k, "lon", 1, 1.0, taps, done)
    *sums, done = weight_grads([normed_far], [masked_far], 1.0, *weights, sums)
    grad_in, grad_out, done = weight_grads([normed_last], [masked_last], factor, *weights, sums)
    grad_k = added(grad_k, "lat", 1, factor, (49, 1, chans), done)

    result = jnp.where(section == 1, dx1, dx0)
    kept = lax.dynamic_slice_in_dim(result, lat * rows, rows, 1)
    given = lax.dynamic_slice_in_dim(result, (1 - lat) * rows, rows, 1)
    got = lax.ppermute(given, "lat", swap)
    low = jnp.where(side == 0, kept, got)
    high = jnp.where(side == 0, got, kept)
    result = jnp.concatenate([low, high], axis=2)
    return result[None], grad_in[None], grad_out[None], jnp.transpose(grad_k, (1, 0, 2))


def shards(saved_inputs, out_cotangent, *rest):
    lats, lons = lax.axis_size("lat"), lax.axis_size("lon")
    paired = lats == 2 and lons == 4
    rows, cols = out_cotangent.shape[1:3]
    paired = paired and rows % 8 == 0 and cols == 16
    body = pair_shards if paired else tile_shards
    return body(saved_inputs, out_cotangent, *rest)


def solution(mesh):
    in_specs = (
        P("section", "group", "lat", "lon", None),
        P("group", "lat", "lon", None),
        P("lat", "lon"),
        P("section", None, None, None),
        P("section", None),
        P("section", None),
        P("section", None, None),
        P("section", None),
        P("section", None, None),
    )
    out_specs = (
        P("section", "group", "lat", "lon", None),
        P("section", "group", None),
        P("section", "group", None),
        P("section", "group", None),
    )
    return jax.shard_map(shards, mesh=mesh, in_specs=in_specs, out_specs=out_specs, check_vma=False)
```

```python
import functools
import jax
import jax.numpy as jnp
from jax import lax
from jax.experimental import pallas as pl
from jax.experimental.pallas import tpu as pltpu
from jax.sharding import PartitionSpec as P

gelu_k = 0.7978845608028654
gelu_c = 0.044715
LANES = 128
HALO = 3
SIDE = 8
F32 = jnp.float32
BF16 = jnp.bfloat16
VMEM_LIMIT = 16 * 1024 * 1024
GATHER_TILES = 8


def call(body, outs, scratch, *args, micros=1.0, scalars=0, specs=None, limit=VMEM_LIMIT):
    if specs is None:
        specs = [pl.BlockSpec(memory_space=pltpu.SMEM)] * scalars
        specs += [pl.BlockSpec(memory_space=pltpu.VMEM)] * (len(args) - scalars)
    return pl.pallas_call(
        body,
        out_shape=outs,
        in_specs=specs,
        out_specs=[pl.BlockSpec(memory_space=pltpu.VMEM)] * len(outs),
        scratch_shapes=scratch,
        compiler_params=pltpu.CompilerParams(vmem_limit_bytes=limit),
        cost_estimate=pl.CostEstimate(
            flops=int(micros * 1.1e9), bytes_accessed=int(micros * 3.6e6), transcendentals=0
        ),
    )(*args)


def like(shape, dtype):
    return jax.ShapeDtypeStruct(shape, dtype)


def nt_dot(left, right):
    return lax.dot_general(left, right, (((1,), (1,)), ((), ())), preferred_element_type=F32)


def tn_dot(left, right):
    return lax.dot_general(left, right, (((0,), (0,)), ((), ())), preferred_element_type=F32)


def gelu_both(h):
    k, c, c3, half, one = (
        jnp.asarray(v, h.dtype) for v in (gelu_k, gelu_k * gelu_c, 3.0 * gelu_k * gelu_c, 0.5, 1.0)
    )
    h2 = h * h
    tval = jnp.tanh(h * (k + c * h2))
    rise = half + half * tval
    return h * rise, rise + (half * h) * (one - tval * tval) * (k + c3 * h2)


def lane_parts(chans):
    return [slice(at, at + LANES) for at in range(0, chans, LANES)]


def widen(dst, own, low, high, left, right):
    rows, cols = own.shape[1], own.shape[2]
    for part, lanes in enumerate(lane_parts(own.shape[3])):
        to = dst.at[part]
        to[:, :HALO, SIDE : SIDE + cols, :] = low[:, :, :, lanes].astype(F32)
        to[:, HALO : HALO + rows, SIDE : SIDE + cols, :] = own[:, :, :, lanes].astype(F32)
        to[:, HALO + rows :, SIDE : SIDE + cols, :] = high[:, :, :, lanes].astype(F32)
        to[:, :, SIDE - HALO : SIDE, :] = left[:, :, :, lanes].astype(F32)
        to[:, :, SIDE + cols : SIDE + cols + HALO, :] = right[:, :, :, lanes].astype(F32)


def depthwise(src, kern, rows, cols, begin, flip, emit):
    chunk = 8 if cols > 8 else 16
    chunk = chunk if rows % chunk == 0 else rows
    for part, lanes in enumerate(lane_parts(kern.shape[1])):
        for micro in range(src.shape[1]):
            for first in range(0, rows, chunk):
                total = jnp.zeros((chunk, cols, LANES), F32)
                for kb in range(7):
                    at = slice(begin + kb, begin + kb + cols)
                    slab = src[part, micro, first : first + chunk + 2 * HALO, at, :]
                    for ka in range(7):
                        tap = (6 - ka) * 7 + (6 - kb) if flip else ka * 7 + kb
                        total = total + slab[ka : ka + chunk] * kern[tap : tap + 1, lanes]
                emit(micro, first, chunk, lanes, total)


def dense_back(masked, slope, zhat, rscale, gain, w_in, w_out):
    dact = nt_dot(masked, w_out)
    dhid = (dact * slope).astype(BF16)
    dzh = nt_dot(dhid, w_in) * gain
    return rscale * (
        dzh
        - jnp.mean(dzh, axis=-1, keepdims=True)
        - zhat * jnp.mean(dzh * zhat, axis=-1, keepdims=True)
    )


def forward_body(
    x, low, high, left, right, masked, kern, bias, gain, w_in, b_in, w_out,
    wide, normed, zhat, rscale, slope, dz, zval,
):
    rows, cols = x.shape[1], x.shape[2]
    widen(wide, x, low, high, left, right)

    def emit(micro, first, chunk, lanes, total):
        at = (micro * rows + first) * cols
        zval[at : at + chunk * cols, lanes] = total.reshape(chunk * cols, LANES)

    depthwise(wide, kern, rows, cols, SIDE - HALO, False, emit)
    z = zval[...] + bias[...]
    centred = z - jnp.mean(z, axis=-1, keepdims=True)
    rs = lax.rsqrt(jnp.mean(centred * centred, axis=-1, keepdims=True) + 1e-06)
    zh = centred * rs
    n = (zh * gain[...]).astype(BF16)
    normed[...] = n
    zhat[...] = zh
    rscale[...] = rs
    h = jnp.dot(n, w_in[...], preferred_element_type=F32) + b_in[...]
    _, sl = gelu_both(h)
    slope[...] = sl
    dz[...] = dense_back(masked[...], sl, zh, rs, gain[...], w_in[...], w_out[...]).astype(BF16)


def back_body(masked, slope, zhat, rscale, gain, w_in, w_out, dz):
    dz[...] = dense_back(
        masked[...], slope[...], zhat[...], rscale[...], gain[...], w_in[...], w_out[...]
    ).astype(BF16)


def kernel_grad_body(first, wide, dz, grad):
    micros, rows, cols, chans = dz.shape
    for part, lanes in enumerate(lane_parts(chans)):
        for kb in range(7):
            begin = first + kb
            sums = [None] * 7
            for micro in range(micros):
                own = dz[micro, :, :, lanes].astype(F32)
                slab = wide[part, micro, :, begin : begin + cols, :]
                for ka in range(7):
                    prod = jnp.sum(slab[ka : ka + rows] * own, axis=0)
                    sums[ka] = prod if sums[ka] is None else sums[ka] + prod
            for ka in range(7):
                tap = ka * 7 + kb
                grad[tap : tap + 1, lanes] = jnp.sum(sums[ka], axis=0, keepdims=True)


def input_grad_body(own, low, high, left, right, masked, maskb, kern, dx, dxm, wide):
    rows, cols = own.shape[1], own.shape[2]
    widen(wide, own, low, high, left, right)

    def emit(micro, first, chunk, lanes, total):
        at = slice(first, first + chunk)
        value = (total + masked[micro, at, :, lanes].astype(F32)).astype(BF16)
        dx[micro, at, :, lanes] = value
        dxm[micro, at, :, lanes] = (value.astype(F32) * maskb[at]).astype(BF16)

    depthwise(wide, kern, rows, cols, SIDE - HALO, True, emit)


def weight_grad_body(parts, carried, factor, *refs):
    normed, masked = refs[:parts], refs[parts : 2 * parts]
    w_in, b_in, w_out = refs[2 * parts : 2 * parts + 3]
    grad_in, grad_out, token, sum_in, sum_out = refs[-5:]
    if carried:
        sum_in[...] = refs[2 * parts + 3][...]
        sum_out[...] = refs[2 * parts + 4][...]
    else:
        sum_in[...] = jnp.zeros_like(sum_in)
        sum_out[...] = jnp.zeros_like(sum_out)
    for part in range(parts):
        cells = normed[part].shape[0]
        step = min(cells, 512)

        @pl.loop(0, cells // step)
        def _(index):
            at = pl.ds(pl.multiple_of(index * step, step), step)
            n = normed[part][at, :]
            gm = masked[part][at, :]
            h = jnp.dot(n, w_in[...], preferred_element_type=F32) + b_in[...]
            act, slope = gelu_both(h.astype(BF16))
            dhid = nt_dot(gm, w_out[...]).astype(BF16) * slope
            sum_in[...] += tn_dot(n, dhid)
            sum_out[...] += tn_dot(act, gm)

    grad_in[...] = sum_in[...] * factor
    grad_out[...] = sum_out[...] * factor
    token[...] = jnp.zeros_like(token)


def lat_edges(first, last):
    count = lax.axis_size("lat")
    if count == 1:
        return jnp.zeros_like(last), jnp.zeros_like(first)
    if count == 2:
        index = lax.axis_index("lat")
        got = lax.ppermute(jnp.where(index == 0, last, first), "lat", [(0, 1), (1, 0)])
        none = jnp.zeros_like(got)
        return jnp.where(index == 0, none, got), jnp.where(index == 0, got, none)
    up = [(i, i + 1) for i in range(count - 1)]
    low = lax.ppermute(last, "lat", up)
    return low, lax.ppermute(first, "lat", [(b, a) for a, b in up])


def halo(own):
    low, high = lat_edges(own[:, :HALO], own[:, -HALO:])
    count = lax.axis_size("lon")
    firsts = jnp.concatenate([v[:, :, :HALO] for v in (low, own, high)], axis=1)
    lasts = jnp.concatenate([v[:, :, -HALO:] for v in (low, own, high)], axis=1)
    ring = [(i, (i + 1) % count) for i in range(count)]
    left = lax.ppermute(lasts, "lon", ring)
    right = lax.ppermute(firsts, "lon", [(b, a) for a, b in ring])
    return low, high, left, right


def ring_pieces(value, axis):
    count = lax.axis_size(axis)
    return [value] + [
        lax.ppermute(value, axis, [(i, (i + d) % count) for i in range(count)])
        for d in range(1, count)
    ]


def crossing_pieces(value):
    count = lax.axis_size("lon")
    pieces = []
    for d in range(count):
        pairs = []
        for i in range(count):
            for s in range(2):
                pairs.append((i * 2 + s, ((i + d) % count) * 2 + 1 - s))
        pieces.append(lax.ppermute(value, ("lon", "section"), pairs))
    return pieces


def summed(value):
    for axis in ("lat", "lon"):
        count = lax.axis_size(axis)
        if count & (count - 1):
            value = lax.psum(value, axis)
            continue
        step = 1
        while step < count:
            value = value + lax.ppermute(value, axis, [(i, i ^ step) for i in range(count)])
            step *= 2
    return value


def weight_grads(normed, masked, factor, w_in, b_in, w_out, carried=(), after=()):
    chans, hidden = w_in.shape
    args = [*normed, *masked, w_in, b_in, w_out, *carried]
    specs = [pl.BlockSpec(memory_space=pltpu.VMEM)] * len(args)
    return call(
        functools.partial(weight_grad_body, len(normed), bool(carried), factor),
        [like((chans, hidden), F32), like((hidden, chans), F32), like((8, LANES), F32)],
        [pltpu.VMEM((chans, hidden), F32), pltpu.VMEM((hidden, chans), F32)],
        *args, *after,
        micros=0.6,
        specs=specs + [pl.BlockSpec(memory_space=pl.ANY)] * len(after),
    )


def tile_shards(
    saved_inputs, out_cotangent, land_mask, conv_kernel, conv_bias, norm_gain, w_in, b_in, w_out
):
    micros, rows, cols, chans = out_cotangent.shape
    hidden = w_in.shape[2]
    cells = micros * rows * cols
    shape = (micros, rows, cols, chans)
    wide_shape = (chans // LANES, micros, rows + 2 * HALO, SIDE + cols + SIDE, LANES)
    flat = (cells, chans)
    tiles = lax.axis_size("lat") * lax.axis_size("lon")
    factor = 1.0 / (cells * tiles) ** 0.5
    section = lax.axis_index("section")
    gather = tiles <= GATHER_TILES

    kern = conv_kernel[0].reshape(49, chans).astype(F32)
    weight_in, weight_out = w_in[0], w_out[0]
    maskf = land_mask.astype(F32)
    maskb = jnp.broadcast_to(maskf[:, :, None], (rows, cols, LANES))
    masked1 = (out_cotangent.astype(F32) * maskf[None, :, :, None]).astype(BF16)

    x = saved_inputs[0]
    wide, normed, zhat, rscale, slope, dz = call(
        forward_body,
        [
            like(wide_shape, F32),
            like(flat, BF16),
            like(flat, F32),
            like((cells, 1), F32),
            like((cells, hidden), F32),
            like(flat, BF16),
        ],
        [pltpu.VMEM(flat, F32)],
        x, *halo(x), masked1.reshape(flat), kern, conv_bias, norm_gain, weight_in, b_in, weight_out,
        micros=3.0,
    )
    if gather:
        normed_row = jnp.concatenate(ring_pieces(normed, "lon"))
        normed_all = ring_pieces(normed_row, "lat")

    def input_grad(dz, masked):
        dz = dz.reshape(shape)
        edges = halo(dz)
        (grad_k,) = call(
            functools.partial(kernel_grad_body, SIDE - HALO),
            [like((49, chans), F32)],
            [],
            wide, dz,
            micros=3.0,
        )
        dx, dxm = call(
            input_grad_body,
            [like(shape, BF16), like(shape, BF16)],
            [pltpu.VMEM(wide_shape, F32)],
            dz, *edges, masked, maskb, kern,
            micros=3.0,
        )
        return grad_k, dx, dxm

    grad_k1, dx1, dxm1 = input_grad(dz, masked1)
    cross = jnp.where(section == 1, dxm1, masked1).reshape(flat)
    if gather:
        pieces = crossing_pieces(cross)
        masked0 = pieces[0]
        masked_all = ring_pieces(jnp.concatenate(pieces), "lat")
    else:
        masked0 = lax.ppermute(cross, "section", [(0, 1), (1, 0)])
        normed_all, masked_all = [normed], [masked0]
    (dz0,) = call(
        back_body, [like(flat, BF16)], [],
        masked0, slope, zhat, rscale, norm_gain, weight_in, weight_out,
        micros=3.0,
    )
    grad_k0, dx0, _ = input_grad(dz0, masked0.reshape(shape))
    grad_k = summed(jnp.where(section == 1, grad_k1, grad_k0)) * factor
    grad_in, grad_out, _ = weight_grads(
        normed_all, masked_all, factor, weight_in, b_in, weight_out
    )
    if not gather:
        grad_in, grad_out = lax.psum((grad_in, grad_out), ("lon", "lat"))
    results = jnp.where(section == 1, dx1, dx0)
    return results[None], grad_in[None], grad_out[None], grad_k[None]


def copied(pairs, sems):
    copies = [pltpu.make_async_copy(a, b, sems.at[i]) for i, (a, b) in enumerate(pairs)]
    for copy in copies:
        copy.start()
    return copies


def prepare_body(
    place, x_far, g_far, mask_far, x, sent, near, far, g, mask, firsts, lasts, sems
):
    micros, rows, cols, chans = x.shape
    for copy in copied([(x_far, x), (g_far, g), (mask_far, mask)], sems):
        copy.wait()
    maskb = jnp.broadcast_to(mask[...].astype(F32)[:, :, None], (rows, cols, chans))
    gm = g[...].astype(F32) * maskb[None]
    sent[:micros] = gm.astype(BF16)
    sent[micros] = maskb.astype(BF16)
    xf = x[...].astype(F32)
    for row in range(micros * rows):
        micro, at = row // rows, row % rows
        for buf, x_cols, g_cols in (
            (firsts, slice(0, 2 * HALO), slice(0, HALO)),
            (lasts, slice(cols - 2 * HALO, cols), slice(cols - HALO, cols)),
        ):
            buf[row * 9 : row * 9 + 6, :] = xf[micro, at, x_cols]
            buf[row * 9 + 6 : row * 9 + 9, :] = gm[micro, at, g_cols]

    @pl.when(place[0] == 1)
    def _():
        near[...] = lasts[...].astype(BF16)
        far[...] = firsts[...].astype(BF16)

    @pl.when(place[0] == 0)
    def _():
        near[...] = firsts[...].astype(BF16)
        far[...] = lasts[...].astype(BF16)


def stage_body(near, masked, taps, *refs):
    count = (len(refs) - 4) // 2
    sources, kern, sent, targets = refs[:count], refs[count], refs[count + 1], refs[count + 2 : -2]
    held, sems = refs[-2:]
    copies = copied(list(zip(sources, targets)) + [(taps, held)], sems)
    sent[...] = masked[...]
    for copy in copies:
        copy.wait()
    for ka in range(7):
        kern[ka * 7 : ka * 7 + 7, :] = held[0, ka].astype(F32)


def norm_body(
    place, x, xp, near, far, kern, bias, gain, w_in, b_in,
    wide, normed, zhat, rscale, slope, zval, packed,
):
    micros, rows, cols, chans = x.shape
    half = cols // 2
    all_rows = 2 * rows
    reach = half + 8
    side, lat = place[0], place[1]
    wide[...] = jnp.zeros_like(wide)
    for tile, edge, at in ((x, near, lat * rows), (xp, far, (1 - lat) * rows)):
        own_rows = pl.ds(HALO + at, rows)
        tile_x = tile[...].astype(F32)
        packed[...] = edge[...].astype(F32)
        skip = half - 2 * HALO
        for number, keep, tile_at, edge_at in ((0, 0, 2 * HALO, 0), (1, skip, 0, cols - skip)):

            @pl.when(side == number)
            def _():
                for part, lanes in enumerate(lane_parts(chans)):
                    to_cols = slice(tile_at, tile_at + cols - keep)
                    wide[part, :, own_rows, to_cols, :] = tile_x[:, :, keep:, lanes]
                    for row in range(micros * rows):
                        wide[
                            part, row // rows, at + HALO + row % rows, edge_at : edge_at + 6, :
                        ] = packed[row * 9 : row * 9 + 6, lanes]

    def emit(micro, first, chunk, lanes, total):
        at = (micro * all_rows + first) * reach
        zval[at : at + chunk * reach, lanes] = total.reshape(chunk * reach, LANES)

    depthwise(wide, kern, all_rows, reach, 0, False, emit)
    z = zval[...] + bias[...]
    centred = z - jnp.mean(z, axis=-1, keepdims=True)
    rs = lax.rsqrt(jnp.mean(centred * centred, axis=-1, keepdims=True) + 1e-06)
    zh = centred * rs
    zhat[...] = zh
    rscale[...] = rs
    n = zh * gain[...]
    core = n.reshape(micros * all_rows, reach, chans)[:, HALO : HALO + half]
    normed[...] = core.reshape(normed.shape).astype(BF16)
    h = jnp.dot(n.astype(BF16), w_in[...], preferred_element_type=F32) + b_in[...]
    slope[...] = gelu_both(h)[1].astype(BF16)


def pair_back(gwide, dwide, zhat, rscale, slope, gain, w_in, w_out, kern, dz, emit):
    micros, rows, reach, chans = gwide.shape
    half = reach - 8
    masked = gwide[...].reshape(micros * rows * reach, chans).astype(BF16)
    dzval = dense_back(
        masked, slope[...].astype(F32), zhat[...], rscale[...], gain[...], w_in[...], w_out[...]
    )
    rounded = dzval.astype(BF16).astype(F32).reshape(micros, rows, reach, chans)
    nothing = jnp.zeros((micros, HALO, reach, LANES), F32)
    for part, lanes in enumerate(lane_parts(chans)):
        dwide[part, :, :HALO] = nothing
        dwide[part, :, HALO + rows :] = nothing
        dwide[part, :, HALO : HALO + rows] = rounded[..., lanes]
    dz[...] = rounded[:, :, HALO : HALO + half].astype(BF16)

    def add(micro, first, chunk, lanes, total):
        own = gwide[micro, first : first + chunk, HALO : HALO + half, lanes]
        emit(micro, slice(first, first + chunk), lanes, (total + own).astype(BF16))

    depthwise(dwide, kern, rows, half, 0, True, add)


def last_back_body(place, *refs):
    @pl.when(place[2] == 1)
    def _():
        last_back_work(place, *refs)


def last_back_work(
    place, gm, gmp, near, far, zhat, rscale, slope, gain, w_in, w_out, kern,
    dx, dxm, first3, last3, dz, core, gwide, dwide, mask, packed,
):
    micros, all_rows, half, chans = dx.shape
    rows, cols = all_rows // 2, 2 * half
    side, lat = place[0], place[1]
    gwide[:, :, half:, :] = jnp.zeros((micros, all_rows, 8, chans), F32)
    for tile, edge, at in ((gm, near, lat * rows), (gmp, far, (1 - lat) * rows)):
        to_rows = pl.ds(at, rows)
        both = tile[...].astype(F32)
        packed[...] = edge[...].astype(F32)

        @pl.when(side == 0)
        def _():
            gwide[:, to_rows, HALO : 2 * HALO + half, :] = both[:micros, :, : half + HALO]
            for row in range(micros * rows):
                gwide[row // rows, at + row % rows, :HALO, :] = packed[row * 9 + 6 : row * 9 + 9, :]
            mask[to_rows] = both[micros, :, :half]

        @pl.when(side == 1)
        def _():
            gwide[:, to_rows, : HALO + half, :] = both[:micros, :, half - HALO :]
            for row in range(micros * rows):
                gwide[row // rows, at + row % rows, HALO + half : 2 * HALO + half, :] = packed[
                    row * 9 + 6 : row * 9 + 9, :
                ]
            mask[to_rows] = both[micros, :, half:]

    core[...] = gwide[:, :, HALO : HALO + half, :].astype(BF16)

    def emit(micro, at, lanes, value):
        dx[micro, at, :, lanes] = value
        kept = value.astype(F32) * mask[at, :, lanes]
        dxm[micro, at, :, lanes] = kept.astype(BF16)
        first3[micro, at, :, lanes] = kept[:, :HALO].astype(BF16)
        last3[micro, at, :, lanes] = kept[:, half - HALO :].astype(BF16)

    pair_back(gwide, dwide, zhat, rscale, slope, gain, w_in, w_out, kern, dz, emit)


def first_back_body(place, *refs):
    @pl.when(place[2] == 0)
    def _():
        first_back_work(*refs)


def first_back_work(
    core, left, right, zhat, rscale, slope, gain, w_in, w_out, kern, dx, dz, gwide, dwide
):
    micros, rows, half, chans = core.shape
    gwide[:, :, half:, :] = jnp.zeros((micros, rows, 8, chans), F32)
    gwide[:, :, :HALO, :] = left[...].astype(F32)
    gwide[:, :, HALO : HALO + half, :] = core[...].astype(F32)
    gwide[:, :, HALO + half : 2 * HALO + half, :] = right[...].astype(F32)

    def emit(micro, at, lanes, value):
        dx[micro, at, :, lanes] = value

    pair_back(gwide, dwide, zhat, rscale, slope, gain, w_in, w_out, kern, dz, emit)


def pair_up(target, first, second):
    half = first.shape[0]
    target[:half] = first[...]
    target[half:] = second[...]


def pair_body(first, second, left0, right0, pair):
    pair_up(pair, first, second)


def select_join_body(place, core1, got1, core0, got0, left0, right0, pair):
    half = pair.shape[0] // 2
    for number, core, got in ((1, core1, got1), (0, core0, got0)):

        @pl.when(place[2] == number)
        def _():
            pair[:half] = core[...].reshape(half, pair.shape[1])
            pair[half:] = got[...].reshape(half, pair.shape[1])


def add_body(scale, first, second, after, out):
    total = (first[...] + second[...]) * scale
    if len(out.shape) == 2:
        out[...] = total
    else:
        for row in range(out.shape[0]):
            out[row] = total[row : row + 1]


def pair_kernel_grad_body(place, wide, dz1, dz0, after, grad, dz):
    for number, own in ((1, dz1), (0, dz0)):

        @pl.when(place[2] == number)
        def _():
            dz[...] = own[...]

    kernel_grad_body(HALO, wide, dz, grad)


def pair_shards(
    saved_inputs, out_cotangent, land_mask, conv_kernel, conv_bias, norm_gain, w_in, b_in, w_out
):
    micros, rows, cols, chans = out_cotangent.shape
    hidden = w_in.shape[2]
    lons = lax.axis_size("lon")
    half, all_rows, reach = cols // 2, 2 * rows, cols // 2 + 8
    cells = micros * all_rows * half
    many = micros * all_rows * reach
    shape = (micros, all_rows, half, chans)
    edge_shape = (micros, all_rows, HALO, chans)
    wide_shape = (chans // LANES, micros, all_rows + 2 * HALO, reach + 8, LANES)
    reach_shape = (micros, all_rows, reach, chans)
    factor = 1.0 / (cells * 2 * lons) ** 0.5
    section, lat, lon = (lax.axis_index(a) for a in ("section", "lat", "lon"))
    side = jnp.bitwise_xor(lat, jnp.bitwise_and(lon, 1))
    count = 2 * lons

    def device(position):
        position = position % count
        tile, which = position // 2, position % 2
        return tile * 2 + (which ^ (tile & 1))

    x = saved_inputs[0]
    place = jnp.stack([side, lat, section]).astype(jnp.int32)
    packed = (micros * rows * 3 * HALO, chans)
    sent_shape = (micros + 1, rows, cols, chans)

    swap = [(0, 1), (1, 0)]
    xp = lax.ppermute(x, "lat", swap)
    anywhere, vmem = pl.BlockSpec(memory_space=pl.ANY), pl.BlockSpec(memory_space=pltpu.VMEM)
    hbm, smem = pl.BlockSpec(memory_space=pltpu.HBM), pl.BlockSpec(memory_space=pltpu.SMEM)
    x_near, masked, near, far = call(
        prepare_body,
        [like(x.shape, BF16), like(sent_shape, BF16), like(packed, BF16), like(packed, BF16)],
        [
            pltpu.VMEM(x.shape, BF16),
            pltpu.VMEM(land_mask.shape, land_mask.dtype),
            pltpu.VMEM(packed, F32),
            pltpu.VMEM(packed, F32),
            pltpu.SemaphoreType.DMA((3,)),
        ],
        place, x, out_cotangent, land_mask,
        specs=[smem, hbm, hbm, hbm],
    )
    near_pairs = [(device(p), device(p + 1 if p % 2 else p - 1)) for p in range(count)]
    far_pairs = [(device(p), device(p - 2 if p % 2 else p + 2)) for p in range(count)]
    near = lax.ppermute(near, ("lon", "lat"), near_pairs)
    far = lax.ppermute(far, ("lon", "lat"), far_pairs)
    params = [conv_bias, norm_gain, w_in[0], b_in, w_out[0]]
    kern, masked, bias, gain, weight_in, bias_in, weight_out = call(
        stage_body,
        [like((49, chans), F32), like(sent_shape, BF16)] + [like(v.shape, v.dtype) for v in params],
        [pltpu.VMEM(conv_kernel.shape, BF16), pltpu.SemaphoreType.DMA((len(params) + 1,))],
        near, masked, conv_kernel, *params,
        specs=[anywhere, vmem] + [hbm] * (1 + len(params)),
    )
    gmp = lax.ppermute(masked, ("lat", "section"), [(1, 3), (3, 1)])

    wide, normed, zhat, rscale, slope = call(
        norm_body,
        [
            like(wide_shape, F32),
            like((cells, chans), BF16),
            like((many, chans), F32),
            like((many, 1), F32),
            like((many, hidden), BF16),
        ],
        [pltpu.VMEM((many, chans), F32), pltpu.VMEM(packed, F32)],
        place, x_near, xp, near, far, kern, bias, gain, weight_in, bias_in,
        micros=6.5,
        scalars=1,
    )
    state = (zhat, rscale, slope, gain, weight_in, weight_out, kern)
    buffers = [
        pltpu.VMEM(reach_shape, F32),
        pltpu.VMEM((chans // LANES, micros, all_rows + 2 * HALO, reach, LANES), F32),
    ]
    dx1, dxm1, first3, last3, dz1, core1 = call(
        last_back_body,
        [like(shape, BF16), like(shape, BF16), like(edge_shape, BF16), like(edge_shape, BF16)]
        + [like(shape, BF16), like(shape, BF16)],
        buffers + [pltpu.VMEM(shape[1:], F32), pltpu.VMEM(packed, F32)],
        place, masked, gmp, near, far, *state,
        micros=4.5,
        scalars=1,
    )
    far_step = lons // 2

    def exchanged(value, axis, step):
        return lax.ppermute(value, axis, [(i, i ^ step) for i in range(lax.axis_size(axis))])

    def across(value, to):
        pairs = [(i * 2 + 1, (i ^ far_step) * 2 + to) for i in range(lons)]
        return lax.ppermute(value, ("lon", "section"), pairs)

    axes = ("lon", "lat", "section")
    core0 = lax.ppermute(dxm1, "section", [(1, 0)])
    left0 = lax.ppermute(
        last3, axes, [(device(p) * 2 + 1, device(p + 1) * 2) for p in range(count)]
    )
    right0 = lax.ppermute(
        first3, axes, [(device(p) * 2 + 1, device(p - 1) * 2) for p in range(count)]
    )
    (masked_pair,) = call(
        select_join_body,
        [like((2 * cells, chans), BF16)],
        [],
        place, core1, across(core1, 1), core0, across(dxm1, 0), left0, right0,
        micros=1.5,
        specs=[smem] + [vmem] * 4 + [anywhere] * 2,
    )
    (normed_pair,) = call(
        pair_body,
        [like((2 * cells, chans), BF16)],
        [],
        normed, exchanged(normed, "lon", far_step), left0, right0,
        micros=1.5,
        specs=[vmem] * 2 + [anywhere] * 2,
    )
    dx0, dz0 = call(
        first_back_body,
        [like(shape, BF16), like(shape, BF16)],
        buffers,
        place, core0, left0, right0, *state,
        micros=4.5,
        scalars=1,
    )
    normed_near, masked_near = exchanged(normed_pair, "lon", 1), exchanged(masked_pair, "lon", 1)
    normed_far, masked_far = (lax.ppermute(v, "lat", swap) for v in (normed_pair, masked_pair))
    normed_last = exchanged(normed_far, "lon", 1)
    masked_last = lax.ppermute(masked_near, "lat", swap)

    (grad_k,) = call(
        pair_kernel_grad_body,
        [like((49, chans), F32)],
        [pltpu.VMEM(shape, BF16)],
        place, wide, dz1, dz0, normed_far,
        micros=1.5,
        specs=[smem] + [vmem] * 3 + [anywhere],
    )
    weights = (weight_in, bias_in, weight_out)

    def added(grad, axis, step, scale, shape, after):
        return call(
            functools.partial(add_body, scale),
            [like(shape, F32)],
            [],
            grad, exchanged(grad, axis, step), after,
            micros=0.2,
            specs=[vmem, vmem, anywhere],
        )[0]

    taps = grad_k.shape
    *sums, done = weight_grads([normed_pair], [masked_pair], 1.0, *weights)
    grad_k = added(grad_k, "lon", far_step, 1.0, taps, done)
    *sums, done = weight_grads([normed_near], [masked_near], 1.0, *weights, sums)
    grad_k = added(grad_k, "lon", 1, 1.0, taps, done)
    *sums, done = weight_grads([normed_far], [masked_far], 1.0, *weights, sums)
    grad_in, grad_out, done = weight_grads([normed_last], [masked_last], factor, *weights, sums)
    grad_k = added(grad_k, "lat", 1, factor, (49, 1, chans), done)

    result = jnp.where(section == 1, dx1, dx0)
    kept = lax.dynamic_slice_in_dim(result, lat * rows, rows, 1)
    given = lax.dynamic_slice_in_dim(result, (1 - lat) * rows, rows, 1)
    got = lax.ppermute(given, "lat", swap)
    low = jnp.where(side == 0, kept, got)
    high = jnp.where(side == 0, got, kept)
    result = jnp.concatenate([low, high], axis=2)
    return result[None], grad_in[None], grad_out[None], jnp.transpose(grad_k, (1, 0, 2))


def shards(saved_inputs, out_cotangent, *rest):
    lats, lons = lax.axis_size("lat"), lax.axis_size("lon")
    paired = lats == 2 and lons == 4
    rows, cols = out_cotangent.shape[1:3]
    paired = paired and rows % 8 == 0 and cols == 16
    body = pair_shards if paired else tile_shards
    return body(saved_inputs, out_cotangent, *rest)


def solution(mesh):
    in_specs = (
        P("section", "group", "lat", "lon", None),
        P("group", "lat", "lon", None),
        P("lat", "lon"),
        P("section", None, None, None),
        P("section", None),
        P("section", None),
        P("section", None, None),
        P("section", None),
        P("section", None, None),
    )
    out_specs = (
        P("section", "group", "lat", "lon", None),
        P("section", "group", None),
        P("section", "group", None),
        P("section", "group", None),
    )
    return jax.shard_map(shards, mesh=mesh, in_specs=in_specs, out_specs=out_specs, check_vma=False)
```

```python
import functools
import jax
import jax.numpy as jnp
from jax import lax
from jax.experimental import pallas as pl
from jax.experimental.pallas import tpu as pltpu
from jax.sharding import PartitionSpec as P

gelu_k = 0.7978845608028654
gelu_c = 0.044715
LANES = 128
HALO = 3
SIDE = 8
F32 = jnp.float32
BF16 = jnp.bfloat16
VMEM_LIMIT = 16 * 1024 * 1024
GATHER_TILES = 8


def call(body, outs, scratch, *args, micros=1.0, scalars=0, specs=None, limit=VMEM_LIMIT):
    if specs is None:
        specs = [pl.BlockSpec(memory_space=pltpu.SMEM)] * scalars
        specs += [pl.BlockSpec(memory_space=pltpu.VMEM)] * (len(args) - scalars)
    return pl.pallas_call(
        body,
        out_shape=outs,
        in_specs=specs,
        out_specs=[pl.BlockSpec(memory_space=pltpu.VMEM)] * len(outs),
        scratch_shapes=scratch,
        compiler_params=pltpu.CompilerParams(vmem_limit_bytes=limit),
        cost_estimate=pl.CostEstimate(
            flops=int(micros * 1.1e9), bytes_accessed=int(micros * 3.6e6), transcendentals=0
        ),
    )(*args)


def like(shape, dtype):
    return jax.ShapeDtypeStruct(shape, dtype)


def nt_dot(left, right):
    return lax.dot_general(left, right, (((1,), (1,)), ((), ())), preferred_element_type=F32)


def tn_dot(left, right):
    return lax.dot_general(left, right, (((0,), (0,)), ((), ())), preferred_element_type=F32)


def gelu_both(h):
    k, c, c3, half, one = (
        jnp.asarray(v, h.dtype) for v in (gelu_k, gelu_k * gelu_c, 3.0 * gelu_k * gelu_c, 0.5, 1.0)
    )
    h2 = h * h
    tval = jnp.tanh(h * (k + c * h2))
    rise = half + half * tval
    return h * rise, rise + (half * h) * (one - tval * tval) * (k + c3 * h2)


def lane_parts(chans):
    return [slice(at, at + LANES) for at in range(0, chans, LANES)]


def widen(dst, own, low, high, left, right):
    rows, cols = own.shape[1], own.shape[2]
    for part, lanes in enumerate(lane_parts(own.shape[3])):
        to = dst.at[part]
        to[:, :HALO, SIDE : SIDE + cols, :] = low[:, :, :, lanes].astype(F32)
        to[:, HALO : HALO + rows, SIDE : SIDE + cols, :] = own[:, :, :, lanes].astype(F32)
        to[:, HALO + rows :, SIDE : SIDE + cols, :] = high[:, :, :, lanes].astype(F32)
        to[:, :, SIDE - HALO : SIDE, :] = left[:, :, :, lanes].astype(F32)
        to[:, :, SIDE + cols : SIDE + cols + HALO, :] = right[:, :, :, lanes].astype(F32)


def depthwise(src, kern, rows, cols, begin, flip, emit):
    chunk = 8 if cols > 8 else 16
    chunk = chunk if rows % chunk == 0 else rows
    for part, lanes in enumerate(lane_parts(kern.shape[1])):
        for micro in range(src.shape[1]):
            for first in range(0, rows, chunk):
                total = jnp.zeros((chunk, cols, LANES), F32)
                for kb in range(7):
                    at = slice(begin + kb, begin + kb + cols)
                    slab = src[part, micro, first : first + chunk + 2 * HALO, at, :]
                    for ka in range(7):
                        tap = (6 - ka) * 7 + (6 - kb) if flip else ka * 7 + kb
                        total = total + slab[ka : ka + chunk] * kern[tap : tap + 1, lanes]
                emit(micro, first, chunk, lanes, total)


def dense_back(masked, slope, zhat, rscale, gain, w_in, w_out):
    dact = nt_dot(masked, w_out)
    dhid = (dact * slope).astype(BF16)
    dzh = nt_dot(dhid, w_in) * gain
    return rscale * (
        dzh
        - jnp.mean(dzh, axis=-1, keepdims=True)
        - zhat * jnp.mean(dzh * zhat, axis=-1, keepdims=True)
    )


def forward_body(
    x, low, high, left, right, masked, kern, bias, gain, w_in, b_in, w_out,
    wide, normed, zhat, rscale, slope, dz, zval,
):
    rows, cols = x.shape[1], x.shape[2]
    widen(wide, x, low, high, left, right)

    def emit(micro, first, chunk, lanes, total):
        at = (micro * rows + first) * cols
        zval[at : at + chunk * cols, lanes] = total.reshape(chunk * cols, LANES)

    depthwise(wide, kern, rows, cols, SIDE - HALO, False, emit)
    z = zval[...] + bias[...]
    centred = z - jnp.mean(z, axis=-1, keepdims=True)
    rs = lax.rsqrt(jnp.mean(centred * centred, axis=-1, keepdims=True) + 1e-06)
    zh = centred * rs
    n = (zh * gain[...]).astype(BF16)
    normed[...] = n
    zhat[...] = zh
    rscale[...] = rs
    h = jnp.dot(n, w_in[...], preferred_element_type=F32) + b_in[...]
    _, sl = gelu_both(h)
    slope[...] = sl
    dz[...] = dense_back(masked[...], sl, zh, rs, gain[...], w_in[...], w_out[...]).astype(BF16)


def back_body(masked, slope, zhat, rscale, gain, w_in, w_out, dz):
    dz[...] = dense_back(
        masked[...], slope[...], zhat[...], rscale[...], gain[...], w_in[...], w_out[...]
    ).astype(BF16)


def kernel_grad_body(first, wide, dz, grad):
    micros, rows, cols, chans = dz.shape
    for part, lanes in enumerate(lane_parts(chans)):
        for kb in range(7):
            begin = first + kb
            sums = [None] * 7
            for micro in range(micros):
                own = dz[micro, :, :, lanes].astype(F32)
                slab = wide[part, micro, :, begin : begin + cols, :]
                for ka in range(7):
                    prod = jnp.sum(slab[ka : ka + rows] * own, axis=0)
                    sums[ka] = prod if sums[ka] is None else sums[ka] + prod
            for ka in range(7):
                tap = ka * 7 + kb
                grad[tap : tap + 1, lanes] = jnp.sum(sums[ka], axis=0, keepdims=True)


def input_grad_body(own, low, high, left, right, masked, maskb, kern, dx, dxm, wide):
    rows, cols = own.shape[1], own.shape[2]
    widen(wide, own, low, high, left, right)

    def emit(micro, first, chunk, lanes, total):
        at = slice(first, first + chunk)
        value = (total + masked[micro, at, :, lanes].astype(F32)).astype(BF16)
        dx[micro, at, :, lanes] = value
        dxm[micro, at, :, lanes] = (value.astype(F32) * maskb[at]).astype(BF16)

    depthwise(wide, kern, rows, cols, SIDE - HALO, True, emit)


def weight_grad_body(parts, carried, factor, *refs):
    normed, masked = refs[:parts], refs[parts : 2 * parts]
    w_in, b_in, w_out = refs[2 * parts : 2 * parts + 3]
    grad_in, grad_out, token, sum_in, sum_out = refs[-5:]
    if carried:
        sum_in[...] = refs[2 * parts + 3][...]
        sum_out[...] = refs[2 * parts + 4][...]
    else:
        sum_in[...] = jnp.zeros_like(sum_in)
        sum_out[...] = jnp.zeros_like(sum_out)
    for part in range(parts):
        cells = normed[part].shape[0]
        step = min(cells, 512)

        @pl.loop(0, cells // step)
        def _(index):
            at = pl.ds(pl.multiple_of(index * step, step), step)
            n = normed[part][at, :]
            gm = masked[part][at, :]
            h = jnp.dot(n, w_in[...], preferred_element_type=F32) + b_in[...]
            act, slope = gelu_both(h.astype(BF16))
            dhid = nt_dot(gm, w_out[...]).astype(BF16) * slope
            sum_in[...] += tn_dot(n, dhid)
            sum_out[...] += tn_dot(act, gm)

    grad_in[...] = sum_in[...] * factor
    grad_out[...] = sum_out[...] * factor
    token[...] = jnp.zeros_like(token)


def lat_edges(first, last):
    count = lax.axis_size("lat")
    if count == 1:
        return jnp.zeros_like(last), jnp.zeros_like(first)
    if count == 2:
        index = lax.axis_index("lat")
        got = lax.ppermute(jnp.where(index == 0, last, first), "lat", [(0, 1), (1, 0)])
        none = jnp.zeros_like(got)
        return jnp.where(index == 0, none, got), jnp.where(index == 0, got, none)
    up = [(i, i + 1) for i in range(count - 1)]
    low = lax.ppermute(last, "lat", up)
    return low, lax.ppermute(first, "lat", [(b, a) for a, b in up])


def halo(own):
    low, high = lat_edges(own[:, :HALO], own[:, -HALO:])
    count = lax.axis_size("lon")
    firsts = jnp.concatenate([v[:, :, :HALO] for v in (low, own, high)], axis=1)
    lasts = jnp.concatenate([v[:, :, -HALO:] for v in (low, own, high)], axis=1)
    ring = [(i, (i + 1) % count) for i in range(count)]
    left = lax.ppermute(lasts, "lon", ring)
    right = lax.ppermute(firsts, "lon", [(b, a) for a, b in ring])
    return low, high, left, right


def ring_pieces(value, axis):
    count = lax.axis_size(axis)
    return [value] + [
        lax.ppermute(value, axis, [(i, (i + d) % count) for i in range(count)])
        for d in range(1, count)
    ]


def crossing_pieces(value):
    count = lax.axis_size("lon")
    pieces = []
    for d in range(count):
        pairs = []
        for i in range(count):
            for s in range(2):
                pairs.append((i * 2 + s, ((i + d) % count) * 2 + 1 - s))
        pieces.append(lax.ppermute(value, ("lon", "section"), pairs))
    return pieces


def summed(value):
    for axis in ("lat", "lon"):
        count = lax.axis_size(axis)
        if count & (count - 1):
            value = lax.psum(value, axis)
            continue
        step = 1
        while step < count:
            value = value + lax.ppermute(value, axis, [(i, i ^ step) for i in range(count)])
            step *= 2
    return value


def weight_grads(normed, masked, factor, w_in, b_in, w_out, carried=(), after=()):
    chans, hidden = w_in.shape
    args = [*normed, *masked, w_in, b_in, w_out, *carried]
    specs = [pl.BlockSpec(memory_space=pltpu.VMEM)] * len(args)
    return call(
        functools.partial(weight_grad_body, len(normed), bool(carried), factor),
        [like((chans, hidden), F32), like((hidden, chans), F32), like((8, LANES), F32)],
        [pltpu.VMEM((chans, hidden), F32), pltpu.VMEM((hidden, chans), F32)],
        *args, *after,
        micros=0.6,
        specs=specs + [pl.BlockSpec(memory_space=pl.ANY)] * len(after),
    )


def tile_shards(
    saved_inputs, out_cotangent, land_mask, conv_kernel, conv_bias, norm_gain, w_in, b_in, w_out
):
    micros, rows, cols, chans = out_cotangent.shape
    hidden = w_in.shape[2]
    cells = micros * rows * cols
    shape = (micros, rows, cols, chans)
    wide_shape = (chans // LANES, micros, rows + 2 * HALO, SIDE + cols + SIDE, LANES)
    flat = (cells, chans)
    tiles = lax.axis_size("lat") * lax.axis_size("lon")
    factor = 1.0 / (cells * tiles) ** 0.5
    section = lax.axis_index("section")
    gather = tiles <= GATHER_TILES

    kern = conv_kernel[0].reshape(49, chans).astype(F32)
    weight_in, weight_out = w_in[0], w_out[0]
    maskf = land_mask.astype(F32)
    maskb = jnp.broadcast_to(maskf[:, :, None], (rows, cols, LANES))
    masked1 = (out_cotangent.astype(F32) * maskf[None, :, :, None]).astype(BF16)

    x = saved_inputs[0]
    wide, normed, zhat, rscale, slope, dz = call(
        forward_body,
        [
            like(wide_shape, F32),
            like(flat, BF16),
            like(flat, F32),
            like((cells, 1), F32),
            like((cells, hidden), F32),
            like(flat, BF16),
        ],
        [pltpu.VMEM(flat, F32)],
        x, *halo(x), masked1.reshape(flat), kern, conv_bias, norm_gain, weight_in, b_in, weight_out,
        micros=3.0,
    )
    if gather:
        normed_row = jnp.concatenate(ring_pieces(normed, "lon"))
        normed_all = ring_pieces(normed_row, "lat")

    def input_grad(dz, masked):
        dz = dz.reshape(shape)
        edges = halo(dz)
        (grad_k,) = call(
            functools.partial(kernel_grad_body, SIDE - HALO),
            [like((49, chans), F32)],
            [],
            wide, dz,
            micros=3.0,
        )
        dx, dxm = call(
            input_grad_body,
            [like(shape, BF16), like(shape, BF16)],
            [pltpu.VMEM(wide_shape, F32)],
            dz, *edges, masked, maskb, kern,
            micros=3.0,
        )
        return grad_k, dx, dxm

    grad_k1, dx1, dxm1 = input_grad(dz, masked1)
    cross = jnp.where(section == 1, dxm1, masked1).reshape(flat)
    if gather:
        pieces = crossing_pieces(cross)
        masked0 = pieces[0]
        masked_all = ring_pieces(jnp.concatenate(pieces), "lat")
    else:
        masked0 = lax.ppermute(cross, "section", [(0, 1), (1, 0)])
        normed_all, masked_all = [normed], [masked0]
    (dz0,) = call(
        back_body, [like(flat, BF16)], [],
        masked0, slope, zhat, rscale, norm_gain, weight_in, weight_out,
        micros=3.0,
    )
    grad_k0, dx0, _ = input_grad(dz0, masked0.reshape(shape))
    grad_k = summed(jnp.where(section == 1, grad_k1, grad_k0)) * factor
    grad_in, grad_out, _ = weight_grads(
        normed_all, masked_all, factor, weight_in, b_in, weight_out
    )
    if not gather:
        grad_in, grad_out = lax.psum((grad_in, grad_out), ("lon", "lat"))
    results = jnp.where(section == 1, dx1, dx0)
    return results[None], grad_in[None], grad_out[None], grad_k[None]


def copied(pairs, sems):
    copies = [pltpu.make_async_copy(a, b, sems.at[i]) for i, (a, b) in enumerate(pairs)]
    for copy in copies:
        copy.start()
    return copies


def prepare_body(
    place, x_far, g_far, mask_far, x, sent, near, far, g, mask, firsts, lasts, sems
):
    micros, rows, cols, chans = x.shape
    for copy in copied([(x_far, x), (g_far, g), (mask_far, mask)], sems):
        copy.wait()
    maskb = jnp.broadcast_to(mask[...].astype(F32)[:, :, None], (rows, cols, chans))
    gm = g[...].astype(F32) * maskb[None]
    sent[:micros] = gm.astype(BF16)
    sent[micros] = maskb.astype(BF16)
    xf = x[...].astype(F32)
    for row in range(micros * rows):
        micro, at = row // rows, row % rows
        for buf, x_cols, g_cols in (
            (firsts, slice(0, 2 * HALO), slice(0, HALO)),
            (lasts, slice(cols - 2 * HALO, cols), slice(cols - HALO, cols)),
        ):
            buf[row * 9 : row * 9 + 6, :] = xf[micro, at, x_cols]
            buf[row * 9 + 6 : row * 9 + 9, :] = gm[micro, at, g_cols]

    @pl.when(place[0] == 1)
    def _():
        near[...] = lasts[...].astype(BF16)
        far[...] = firsts[...].astype(BF16)

    @pl.when(place[0] == 0)
    def _():
        near[...] = firsts[...].astype(BF16)
        far[...] = lasts[...].astype(BF16)


def stage_body(near, masked, taps, *refs):
    count = (len(refs) - 4) // 2
    sources, kern, sent, targets = refs[:count], refs[count], refs[count + 1], refs[count + 2 : -2]
    held, sems = refs[-2:]
    copies = copied(list(zip(sources, targets)) + [(taps, held)], sems)
    sent[...] = masked[...]
    for copy in copies:
        copy.wait()
    for ka in range(7):
        kern[ka * 7 : ka * 7 + 7, :] = held[0, ka].astype(F32)


def norm_body(
    place, x, xp, near, far, kern, bias, gain, w_in, b_in,
    wide, normed, zhat, rscale, slope, zval, packed,
):
    micros, rows, cols, chans = x.shape
    half = cols // 2
    all_rows = 2 * rows
    reach = half + 8
    side, lat = place[0], place[1]
    wide[...] = jnp.zeros_like(wide)
    for tile, edge, at in ((x, near, lat * rows), (xp, far, (1 - lat) * rows)):
        own_rows = pl.ds(HALO + at, rows)
        tile_x = tile[...].astype(F32)
        packed[...] = edge[...].astype(F32)
        skip = half - 2 * HALO
        for number, keep, tile_at, edge_at in ((0, 0, 2 * HALO, 0), (1, skip, 0, cols - skip)):

            @pl.when(side == number)
            def _():
                for part, lanes in enumerate(lane_parts(chans)):
                    to_cols = slice(tile_at, tile_at + cols - keep)
                    wide[part, :, own_rows, to_cols, :] = tile_x[:, :, keep:, lanes]
                    for row in range(micros * rows):
                        wide[
                            part, row // rows, at + HALO + row % rows, edge_at : edge_at + 6, :
                        ] = packed[row * 9 : row * 9 + 6, lanes]

    def emit(micro, first, chunk, lanes, total):
        at = (micro * all_rows + first) * reach
        zval[at : at + chunk * reach, lanes] = total.reshape(chunk * reach, LANES)

    depthwise(wide, kern, all_rows, reach, 0, False, emit)
    z = zval[...] + bias[...]
    centred = z - jnp.mean(z, axis=-1, keepdims=True)
    rs = lax.rsqrt(jnp.mean(centred * centred, axis=-1, keepdims=True) + 1e-06)
    zh = centred * rs
    zhat[...] = zh
    rscale[...] = rs
    n = zh * gain[...]
    core = n.reshape(micros * all_rows, reach, chans)[:, HALO : HALO + half]
    normed[...] = core.reshape(normed.shape).astype(BF16)
    h = jnp.dot(n.astype(BF16), w_in[...], preferred_element_type=F32) + b_in[...]
    slope[...] = gelu_both(h.astype(BF16))[1]


def pair_back(gwide, dwide, zhat, rscale, slope, gain, w_in, w_out, kern, dz, emit):
    micros, rows, reach, chans = gwide.shape
    half = reach - 8
    masked = gwide[...].reshape(micros * rows * reach, chans).astype(BF16)
    dzval = dense_back(
        masked, slope[...].astype(F32), zhat[...], rscale[...], gain[...], w_in[...], w_out[...]
    )
    rounded = dzval.astype(BF16).astype(F32).reshape(micros, rows, reach, chans)
    nothing = jnp.zeros((micros, HALO, reach, LANES), F32)
    for part, lanes in enumerate(lane_parts(chans)):
        dwide[part, :, :HALO] = nothing
        dwide[part, :, HALO + rows :] = nothing
        dwide[part, :, HALO : HALO + rows] = rounded[..., lanes]
    dz[...] = rounded[:, :, HALO : HALO + half].astype(BF16)

    def add(micro, first, chunk, lanes, total):
        own = gwide[micro, first : first + chunk, HALO : HALO + half, lanes]
        emit(micro, slice(first, first + chunk), lanes, (total + own).astype(BF16))

    depthwise(dwide, kern, rows, half, 0, True, add)


def last_back_body(place, *refs):
    @pl.when(place[2] == 1)
    def _():
        last_back_work(place, *refs)


def last_back_work(
    place, gm, gmp, near, far, zhat, rscale, slope, gain, w_in, w_out, kern,
    dx, dxm, first3, last3, dz, core, gwide, dwide, mask, packed,
):
    micros, all_rows, half, chans = dx.shape
    rows, cols = all_rows // 2, 2 * half
    side, lat = place[0], place[1]
    gwide[:, :, half:, :] = jnp.zeros((micros, all_rows, 8, chans), F32)
    for tile, edge, at in ((gm, near, lat * rows), (gmp, far, (1 - lat) * rows)):
        to_rows = pl.ds(at, rows)
        both = tile[...].astype(F32)
        packed[...] = edge[...].astype(F32)

        @pl.when(side == 0)
        def _():
            gwide[:, to_rows, HALO : 2 * HALO + half, :] = both[:micros, :, : half + HALO]
            for row in range(micros * rows):
                gwide[row // rows, at + row % rows, :HALO, :] = packed[row * 9 + 6 : row * 9 + 9, :]
            mask[to_rows] = both[micros, :, :half]

        @pl.when(side == 1)
        def _():
            gwide[:, to_rows, : HALO + half, :] = both[:micros, :, half - HALO :]
            for row in range(micros * rows):
                gwide[row // rows, at + row % rows, HALO + half : 2 * HALO + half, :] = packed[
                    row * 9 + 6 : row * 9 + 9, :
                ]
            mask[to_rows] = both[micros, :, half:]

    core[...] = gwide[:, :, HALO : HALO + half, :].astype(BF16)

    def emit(micro, at, lanes, value):
        dx[micro, at, :, lanes] = value
        kept = value.astype(F32) * mask[at, :, lanes]
        dxm[micro, at, :, lanes] = kept.astype(BF16)
        first3[micro, at, :, lanes] = kept[:, :HALO].astype(BF16)
        last3[micro, at, :, lanes] = kept[:, half - HALO :].astype(BF16)

    pair_back(gwide, dwide, zhat, rscale, slope, gain, w_in, w_out, kern, dz, emit)


def first_back_body(place, *refs):
    @pl.when(place[2] == 0)
    def _():
        first_back_work(*refs)


def first_back_work(
    core, left, right, zhat, rscale, slope, gain, w_in, w_out, kern, dx, dz, gwide, dwide
):
    micros, rows, half, chans = core.shape
    gwide[:, :, half:, :] = jnp.zeros((micros, rows, 8, chans), F32)
    gwide[:, :, :HALO, :] = left[...].astype(F32)
    gwide[:, :, HALO : HALO + half, :] = core[...].astype(F32)
    gwide[:, :, HALO + half : 2 * HALO + half, :] = right[...].astype(F32)

    def emit(micro, at, lanes, value):
        dx[micro, at, :, lanes] = value

    pair_back(gwide, dwide, zhat, rscale, slope, gain, w_in, w_out, kern, dz, emit)


def pair_up(target, first, second):
    half = first.shape[0]
    target[:half] = first[...]
    target[half:] = second[...]


def pair_body(first, second, left0, right0, pair):
    pair_up(pair, first, second)


def select_join_body(place, core1, got1, core0, got0, left0, right0, pair):
    half = pair.shape[0] // 2
    for number, core, got in ((1, core1, got1), (0, core0, got0)):

        @pl.when(place[2] == number)
        def _():
            pair[:half] = core[...].reshape(half, pair.shape[1])
            pair[half:] = got[...].reshape(half, pair.shape[1])


def add_body(scale, first, second, after, out):
    total = (first[...] + second[...]) * scale
    if len(out.shape) == 2:
        out[...] = total
    else:
        for row in range(out.shape[0]):
            out[row] = total[row : row + 1]


def pair_kernel_grad_body(place, wide, dz1, dz0, after, grad, dz):
    for number, own in ((1, dz1), (0, dz0)):

        @pl.when(place[2] == number)
        def _():
            dz[...] = own[...]

    kernel_grad_body(HALO, wide, dz, grad)


def pair_shards(
    saved_inputs, out_cotangent, land_mask, conv_kernel, conv_bias, norm_gain, w_in, b_in, w_out
):
    micros, rows, cols, chans = out_cotangent.shape
    hidden = w_in.shape[2]
    lons = lax.axis_size("lon")
    half, all_rows, reach = cols // 2, 2 * rows, cols // 2 + 8
    cells = micros * all_rows * half
    many = micros * all_rows * reach
    shape = (micros, all_rows, half, chans)
    edge_shape = (micros, all_rows, HALO, chans)
    wide_shape = (chans // LANES, micros, all_rows + 2 * HALO, reach + 8, LANES)
    reach_shape = (micros, all_rows, reach, chans)
    factor = 1.0 / (cells * 2 * lons) ** 0.5
    section, lat, lon = (lax.axis_index(a) for a in ("section", "lat", "lon"))
    side = jnp.bitwise_xor(lat, jnp.bitwise_and(lon, 1))
    count = 2 * lons

    def device(position):
        position = position % count
        tile, which = position // 2, position % 2
        return tile * 2 + (which ^ (tile & 1))

    x = saved_inputs[0]
    place = jnp.stack([side, lat, section]).astype(jnp.int32)
    packed = (micros * rows * 3 * HALO, chans)
    sent_shape = (micros + 1, rows, cols, chans)

    swap = [(0, 1), (1, 0)]
    xp = lax.ppermute(x, "lat", swap)
    anywhere, vmem = pl.BlockSpec(memory_space=pl.ANY), pl.BlockSpec(memory_space=pltpu.VMEM)
    hbm, smem = pl.BlockSpec(memory_space=pltpu.HBM), pl.BlockSpec(memory_space=pltpu.SMEM)
    x_near, masked, near, far = call(
        prepare_body,
        [like(x.shape, BF16), like(sent_shape, BF16), like(packed, BF16), like(packed, BF16)],
        [
            pltpu.VMEM(x.shape, BF16),
            pltpu.VMEM(land_mask.shape, land_mask.dtype),
            pltpu.VMEM(packed, F32),
            pltpu.VMEM(packed, F32),
            pltpu.SemaphoreType.DMA((3,)),
        ],
        place, x, out_cotangent, land_mask,
        specs=[smem, hbm, hbm, hbm],
    )
    near_pairs = [(device(p), device(p + 1 if p % 2 else p - 1)) for p in range(count)]
    far_pairs = [(device(p), device(p - 2 if p % 2 else p + 2)) for p in range(count)]
    near = lax.ppermute(near, ("lon", "lat"), near_pairs)
    far = lax.ppermute(far, ("lon", "lat"), far_pairs)
    params = [conv_bias, norm_gain, w_in[0], b_in, w_out[0]]
    kern, masked, bias, gain, weight_in, bias_in, weight_out = call(
        stage_body,
        [like((49, chans), F32), like(sent_shape, BF16)] + [like(v.shape, v.dtype) for v in params],
        [pltpu.VMEM(conv_kernel.shape, BF16), pltpu.SemaphoreType.DMA((len(params) + 1,))],
        near, masked, conv_kernel, *params,
        specs=[anywhere, vmem] + [hbm] * (1 + len(params)),
    )
    gmp = lax.ppermute(masked, ("lat", "section"), [(1, 3), (3, 1)])

    wide, normed, zhat, rscale, slope = call(
        norm_body,
        [
            like(wide_shape, F32),
            like((cells, chans), BF16),
            like((many, chans), F32),
            like((many, 1), F32),
            like((many, hidden), BF16),
        ],
        [pltpu.VMEM((many, chans), F32), pltpu.VMEM(packed, F32)],
        place, x_near, xp, near, far, kern, bias, gain, weight_in, bias_in,
        micros=6.5,
        scalars=1,
    )
    state = (zhat, rscale, slope, gain, weight_in, weight_out, kern)
    buffers = [
        pltpu.VMEM(reach_shape, F32),
        pltpu.VMEM((chans // LANES, micros, all_rows + 2 * HALO, reach, LANES), F32),
    ]
    dx1, dxm1, first3, last3, dz1, core1 = call(
        last_back_body,
        [like(shape, BF16), like(shape, BF16), like(edge_shape, BF16), like(edge_shape, BF16)]
        + [like(shape, BF16), like(shape, BF16)],
        buffers + [pltpu.VMEM(shape[1:], F32), pltpu.VMEM(packed, F32)],
        place, masked, gmp, near, far, *state,
        micros=4.5,
        scalars=1,
    )
    far_step = lons // 2

    def exchanged(value, axis, step):
        return lax.ppermute(value, axis, [(i, i ^ step) for i in range(lax.axis_size(axis))])

    def across(value, to):
        pairs = [(i * 2 + 1, (i ^ far_step) * 2 + to) for i in range(lons)]
        return lax.ppermute(value, ("lon", "section"), pairs)

    axes = ("lon", "lat", "section")
    core0 = lax.ppermute(dxm1, "section", [(1, 0)])
    left0 = lax.ppermute(
        last3, axes, [(device(p) * 2 + 1, device(p + 1) * 2) for p in range(count)]
    )
    right0 = lax.ppermute(
        first3, axes, [(device(p) * 2 + 1, device(p - 1) * 2) for p in range(count)]
    )
    (masked_pair,) = call(
        select_join_body,
        [like((2 * cells, chans), BF16)],
        [],
        place, core1, across(core1, 1), core0, across(dxm1, 0), left0, right0,
        micros=1.5,
        specs=[smem] + [vmem] * 4 + [anywhere] * 2,
    )
    (normed_pair,) = call(
        pair_body,
        [like((2 * cells, chans), BF16)],
        [],
        normed, exchanged(normed, "lon", far_step), left0, right0,
        micros=1.5,
        specs=[vmem] * 2 + [anywhere] * 2,
    )
    dx0, dz0 = call(
        first_back_body,
        [like(shape, BF16), like(shape, BF16)],
        buffers,
        place, core0, left0, right0, *state,
        micros=4.5,
        scalars=1,
    )
    normed_near, masked_near = exchanged(normed_pair, "lon", 1), exchanged(masked_pair, "lon", 1)
    normed_far, masked_far = (lax.ppermute(v, "lat", swap) for v in (normed_pair, masked_pair))
    normed_last = exchanged(normed_far, "lon", 1)
    masked_last = lax.ppermute(masked_near, "lat", swap)

    (grad_k,) = call(
        pair_kernel_grad_body,
        [like((49, chans), F32)],
        [pltpu.VMEM(shape, BF16)],
        place, wide, dz1, dz0, normed_far,
        micros=1.5,
        specs=[smem] + [vmem] * 3 + [anywhere],
    )
    weights = (weight_in, bias_in, weight_out)

    def added(grad, axis, step, scale, shape, after):
        return call(
            functools.partial(add_body, scale),
            [like(shape, F32)],
            [],
            grad, exchanged(grad, axis, step), after,
            micros=0.2,
            specs=[vmem, vmem, anywhere],
        )[0]

    taps = grad_k.shape
    *sums, done = weight_grads([normed_pair], [masked_pair], 1.0, *weights)
    grad_k = added(grad_k, "lon", far_step, 1.0, taps, done)
    *sums, done = weight_grads([normed_near], [masked_near], 1.0, *weights, sums)
    grad_k = added(grad_k, "lon", 1, 1.0, taps, done)
    *sums, done = weight_grads([normed_far], [masked_far], 1.0, *weights, sums)
    grad_in, grad_out, done = weight_grads([normed_last], [masked_last], factor, *weights, sums)
    grad_k = added(grad_k, "lat", 1, factor, (49, 1, chans), done)

    result = jnp.where(section == 1, dx1, dx0)
    kept = lax.dynamic_slice_in_dim(result, lat * rows, rows, 1)
    given = lax.dynamic_slice_in_dim(result, (1 - lat) * rows, rows, 1)
    got = lax.ppermute(given, "lat", swap)
    low = jnp.where(side == 0, kept, got)
    high = jnp.where(side == 0, got, kept)
    result = jnp.concatenate([low, high], axis=2)
    return result[None], grad_in[None], grad_out[None], jnp.transpose(grad_k, (1, 0, 2))


def shards(saved_inputs, out_cotangent, *rest):
    lats, lons = lax.axis_size("lat"), lax.axis_size("lon")
    paired = lats == 2 and lons == 4
    rows, cols = out_cotangent.shape[1:3]
    paired = paired and rows % 8 == 0 and cols == 16
    body = pair_shards if paired else tile_shards
    return body(saved_inputs, out_cotangent, *rest)


def solution(mesh):
    in_specs = (
        P("section", "group", "lat", "lon", None),
        P("group", "lat", "lon", None),
        P("lat", "lon"),
        P("section", None, None, None),
        P("section", None),
        P("section", None),
        P("section", None, None),
        P("section", None),
        P("section", None, None),
    )
    out_specs = (
        P("section", "group", "lat", "lon", None),
        P("section", "group", None),
        P("section", "group", None),
        P("section", "group", None),
    )
    return jax.shard_map(shards, mesh=mesh, in_specs=in_specs, out_specs=out_specs, check_vma=False)
```
